32 devices in a mesh: row: 4 (over y, x), col: 8 (over z, core).
Axes of the slice: x: 2, y: 2, z: 4, core: 2. Of those that a mesh axis runs over, the one named last changes fastest.
Arguments:
- query_states: bfloat16 [4, 8, 128, 768], P('row', 'col'), may hold values from -15 to 15
- key_states: bfloat16 [4, 8, 128, 768], P('row', 'col'), may hold values from -6 to 6
- value_states: bfloat16 [4, 8, 128, 768], P('row', 'col'), may hold values from -6 to 6
- tissue_map: int32 [4, 8], replicated, may hold values 0 or 1
Outputs:
- attended: bfloat16 [4, 8, 128, 768], P('row', 'col')
The draws below stay inside these ranges and needn't reach their ends.
All inputs are finite; a program needn't handle non-finite values.
Results may differ from the reference program's by a relative error of at most 0.0032.
Values may be sent and summed in bfloat16 or wider, within the bound.
A program may use at most 64 MiB of HBM per device.

```python
import jax
import jax.numpy as jnp
from jax import lax

HDIM = 64
HEADS = 12
TOK_TILE = 128
TR = 4
TC = 8
HD = 768


def draw_query_states(key, part):
    sample = 2.5 * jax.random.truncated_normal(jax.random.fold_in(key, 1), -6.0, 6.0, (TR, TC, TOK_TILE, HEADS * HDIM))
    return sample.astype(jnp.bfloat16)


def draw_key_states(key, part):
    sample = jax.random.truncated_normal(jax.random.fold_in(key, 2), -6.0, 6.0, (TR, TC, TOK_TILE, HEADS * HDIM))
    return sample.astype(jnp.bfloat16)


def touch_ends(entries, stream_key, least, top_value):
    shape = entries.shape
    place = [jax.random.randint(jax.random.fold_in(stream_key, axis), (), 0, shape[axis]) for axis in range(len(shape))]
    entries = entries.at[tuple(place)].set(least)
    longest = shape.index(max(shape))
    place[longest] = (place[longest] + 1) % shape[longest]
    return entries.at[tuple(place)].set(top_value)


def shard_levels(stream_key, shape, pieces, least, high):
    loudness, own = 1.0, jax.random.fold_in(stream_key, 6)
    for axis_at, shards_of in pieces:
        steps = jnp.exp(jax.random.uniform(jax.random.fold_in(own, axis_at), (shards_of,), jnp.float32, least / len(pieces), high / len(pieces)))
        loudness = loudness * jnp.repeat(steps, shape[axis_at] // shards_of).reshape([-1 if axis == axis_at else 1 for axis in range(len(shape))])
    return loudness


def scatter_about(key, shape, scale, bound, shards=(), kind=jnp.bfloat16):
    array = scale * jax.random.normal(key, shape, jnp.float32)
    if shards:
        array = array * shard_levels(key, shape, shards, -0.22, 0.18)
    return jnp.clip(array, -bound, bound).astype(kind)


def setup_inputs(seed: int = 0) -> dict:
    arg_keys = jax.random.split(jax.random.key(seed), 5)
    return {
        "query_states": draw_query_states(jax.random.fold_in(arg_keys[4], 71), 0),
        "key_states": draw_key_states(jax.random.fold_in(arg_keys[4], 71), 0),
        "value_states": scatter_about(arg_keys[2], (TR, TC, TOK_TILE, HD), 1.0, 6.0, ((0, 4), (1, 8))),
        "tissue_map": touch_ends((jax.random.randint(arg_keys[3], (TR, TC), 0, 4) < 3).astype(jnp.int32), jax.random.fold_in(arg_keys[3], 1), 0, 1),
    }


def reference(query_states, key_states, value_states, tissue_map):
    score_scale = HDIM ** -0.5
    tile_pad = ((1, 1), (1, 1), (0, 0), (0, 0))
    keys_padded = jnp.pad(key_states, tile_pad)
    values_padded = jnp.pad(value_states, tile_pad)
    tissue_padded = jnp.pad(tissue_map, 1)
    centre = jnp.arange(9) == 4

    def one_tile(tile_index):
        row_at = (tile_index // TC).astype(jnp.int32)
        col_at = (tile_index % TC).astype(jnp.int32)
        zero = jnp.zeros((), jnp.int32)
        query_tile = lax.dynamic_slice(query_states, (row_at, col_at, zero, zero), (1, 1, TOK_TILE, HD))
        query_tile = query_tile.reshape(TOK_TILE, HEADS, HDIM).astype(jnp.float32)
        near_keys = lax.dynamic_slice(keys_padded, (row_at, col_at, zero, zero), (3, 3, TOK_TILE, HD))
        near_keys = near_keys.reshape(9 * TOK_TILE, HEADS, HDIM).astype(jnp.float32)
        near_values = lax.dynamic_slice(values_padded, (row_at, col_at, zero, zero), (3, 3, TOK_TILE, HD))
        near_values = near_values.reshape(9 * TOK_TILE, HEADS, HDIM).astype(jnp.float32)
        markers = lax.dynamic_slice(tissue_padded, (row_at, col_at), (3, 3)).reshape(9)
        present = (markers > 0) | centre
        key_keep = jnp.repeat(present, TOK_TILE)
        scores = jnp.einsum("qhd,khd->hqk", query_tile, near_keys) * score_scale
        scores = jnp.where(key_keep[None, None, :], scores, -jnp.inf)
        row_top = jnp.max(scores, axis=-1, keepdims=True)
        weights = jnp.exp(scores - row_top)
        totals = jnp.sum(weights, axis=-1)
        rounded = lax.optimization_barrier(weights.astype(jnp.bfloat16)).astype(jnp.float32)
        mixed = jnp.einsum("hqk,khd->qhd", rounded, near_values)
        mixed = mixed / jnp.transpose(totals)[:, :, None]
        own_tile = markers[4].astype(jnp.float32)
        return (mixed * own_tile).reshape(TOK_TILE, HD).astype(jnp.bfloat16)

    attended = lax.map(one_tile, jnp.arange(TR * TC, dtype=jnp.int32))
    return attended.reshape(TR, TC, TOK_TILE, HD)
```

```python
import functools

import jax
import jax.numpy as jnp
from jax import lax
from jax.experimental import pallas as pl
from jax.experimental.pallas import tpu as pltpu
from jax.sharding import PartitionSpec as P

HDIM = 64
LANES = 128
MESH = pl.DeviceIdType.MESH
LAG = 3


def kernel(rows, cols, tissue, q_hbm, k_hbm, v_hbm, out_ref, kv, qv, bias, local_sem,
           row_send, row_recv, col_send, col_recv):
    chunks, _, _, tokens, _ = kv.shape
    r, c = lax.axis_index("row"), lax.axis_index("col")
    ring = rows == 4
    has_up, has_down = r > 0, r < rows - 1
    has_left, has_right = c > 0, c < cols - 1
    slot = lambda a, b: (a + 1) * 3 + b + 1
    part = lambda i, s: kv.at[i, :, s]

    def lanes(i):
        return pl.ds(pl.multiple_of(i * LANES, LANES), LANES)

    def local_copies(i):
        return [
            pltpu.make_async_copy(k_hbm.at[0, 0, :, lanes(i)], kv.at[i, 0, 4], local_sem.at[0, i]),
            pltpu.make_async_copy(v_hbm.at[0, 0, :, lanes(i)], kv.at[i, 1, 4], local_sem.at[1, i]),
            pltpu.make_async_copy(q_hbm.at[0, 0, :, lanes(i)], qv.at[i], local_sem.at[2, i]),
        ]

    @pl.loop(0, chunks)
    def _(i):
        for copy in local_copies(i):
            copy.start()

    if ring:
        near = 1 - 2 * lax.rem(r, 2)
        outer = jnp.logical_or(r == 0, r == 3)
        inner = jnp.logical_and(r > 0, r < 3)
        across = jnp.where(r < 2, r + 2, r - 2)
        channels = [
            (None, near, None, r + near, slot(0, 0), slot(-near, 0)),
            (inner, -near, outer, across, slot(near, 0), slot(-near, 0)),
        ]
        greet = [(None, r + near), (None, across)]
    else:
        channels = [
            (has_up, -1, has_down, r + 1, slot(0, 0), slot(-1, 0)),
            (has_down, 1, has_up, r - 1, slot(0, 0), slot(1, 0)),
        ]
        greet = [(has_up, r - 1), (has_down, r + 1)]

    def when(cond, f):
        if cond is None:
            f()
        else:
            pl.when(cond)(f)

    barrier = pltpu.get_barrier_semaphore()
    count = 0
    for cond, other in greet:
        when(cond, lambda other=other: pl.semaphore_signal(
            barrier, inc=1, device_id=(other, c), device_id_type=MESH))
        count = count + (1 if cond is None else cond.astype(jnp.int32))
    for cond, other in ((has_left, c - 1), (has_right, c + 1)):
        when(cond, lambda other=other: pl.semaphore_signal(
            barrier, inc=1, device_id=(r, other), device_id_type=MESH))
        count = count + cond.astype(jnp.int32)

    for a in (-1, 0, 1):
        for b in (-1, 0, 1):
            s = slot(a, b)
            if (a, b) == (0, 0):
                bias[:, s * tokens:(s + 1) * tokens] = jnp.zeros((8, tokens), jnp.float32)
                continue
            inside = jnp.logical_and(jnp.logical_and(r + a >= 0, r + a < rows),
                                     jnp.logical_and(c + b >= 0, c + b < cols))
            entry = tissue[jnp.clip(r + a, 0, rows - 1), jnp.clip(c + b, 0, cols - 1)]
            live = jnp.where(inside, entry, 0) > 0
            shift = jnp.where(live, jnp.float32(0), jnp.float32(-jnp.inf))
            bias[:, s * tokens:(s + 1) * tokens] = jnp.full((8, tokens), shift, jnp.float32)

            @pl.when(jnp.logical_not(inside))
            def _():
                @pl.loop(0, chunks)
                def _(i):
                    kv[i, :, s] = jnp.zeros((2, tokens, LANES), kv.dtype)

    pl.semaphore_wait(barrier, count)

    def row_copy(ch, i):
        _, _, _, target, source, landing = channels[ch]
        return pltpu.make_async_remote_copy(
            src_ref=part(i, source), dst_ref=part(i, landing),
            send_sem=row_send.at[ch, i], recv_sem=row_recv.at[ch, i],
            device_id=(target, c), device_id_type=MESH)

    def col_copy(direction, which, i):
        a = 0 if which == 0 else channels[which - 1][1]
        b = -1 if direction == 0 else 1
        return pltpu.make_async_remote_copy(
            src_ref=part(i, slot(a, 0)), dst_ref=part(i, slot(a, b)),
            send_sem=col_send.at[direction, which, i], recv_sem=col_recv.at[direction, which, i],
            device_id=(r, c - b), device_id_type=MESH)

    def col_sends(which, i):
        when(has_right, lambda: col_copy(0, which, i).start())
        when(has_left, lambda: col_copy(1, which, i).start())

    @pl.loop(0, chunks)
    def _(i):
        for copy in local_copies(i):
            copy.wait()
        for ch in (0, 1):
            if not (ring and ch == 1):
                when(channels[ch][2], lambda: row_copy(ch, i).start())
        col_sends(0, i)

    def forward(i):
        for ch in (0, 1):
            def step():
                row_copy(ch, i).wait_recv()
                if ring and ch == 0:
                    when(channels[1][2], lambda: row_copy(1, i).start())
                col_sends(1 + ch, i)
            when(channels[ch][0], step)

    own = tissue[r, c].astype(jnp.float32)
    low = lax.broadcasted_iota(jnp.int32, (tokens, LANES), 1) < HDIM

    def compute(i):
        for direction, cond in ((0, has_left), (1, has_right)):
            for which in (0, 1, 2):
                there = cond
                if which and channels[which - 1][0] is not None:
                    there = jnp.logical_and(cond, channels[which - 1][0])
                when(there, lambda: col_copy(direction, which, i).wait_recv())
        q = qv[i] * jnp.bfloat16(HDIM ** -0.5)
        zero = jnp.zeros_like(q)
        pair = jnp.concatenate([jnp.where(low, q, zero), jnp.where(low, zero, q)], axis=0)
        keys = kv[i, 0].reshape(9 * tokens, LANES)
        values = kv[i, 1].reshape(9 * tokens, LANES)
        scores = lax.dot_general(pair, keys, (((1,), (1,)), ((), ())), preferred_element_type=jnp.float32)
        scores = scores + bias[0:1, :]
        weights = jnp.exp(scores - jnp.max(scores, axis=1, keepdims=True))
        totals = jnp.sum(weights, axis=1, keepdims=True)
        mixed = jnp.dot(weights.astype(jnp.bfloat16), values, preferred_element_type=jnp.float32)
        mixed = mixed / totals * own
        out_ref[0, 0, :, lanes(i)] = jnp.where(low, mixed[:tokens], mixed[tokens:]).astype(out_ref.dtype)

    @pl.loop(0, LAG)
    def _(i):
        forward(i)

    @pl.loop(LAG, chunks)
    def _(i):
        forward(i)
        compute(i - LAG)

    @pl.loop(chunks - LAG, chunks)
    def _(i):
        compute(i)

    @pl.loop(0, chunks)
    def _(i):
        for ch in (0, 1):
            when(channels[ch][2], lambda: row_copy(ch, i).wait_send())
        for which in (0, 1, 2):
            for direction, cond in ((0, has_right), (1, has_left)):
                there = cond
                if which and channels[which - 1][0] is not None:
                    there = jnp.logical_and(cond, channels[which - 1][0])
                when(there, lambda: col_copy(direction, which, i).wait_send())


def on_device(rows, cols, query_states, key_states, value_states, tissue_map):
    _, _, tokens, features = query_states.shape
    chunks = features // LANES
    any_space = pl.BlockSpec(memory_space=pl.ANY)
    return pl.pallas_call(
        functools.partial(kernel, rows, cols),
        out_shape=jax.ShapeDtypeStruct(query_states.shape, jnp.bfloat16),
        in_specs=[pl.BlockSpec(memory_space=pltpu.SMEM), any_space, any_space, any_space],
        out_specs=pl.BlockSpec(memory_space=pltpu.VMEM),
        scratch_shapes=[
            pltpu.VMEM((chunks, 2, 9, tokens, LANES), jnp.bfloat16),
            pltpu.VMEM((chunks, tokens, LANES), jnp.bfloat16),
            pltpu.VMEM((8, 9 * tokens), jnp.float32),
            pltpu.SemaphoreType.DMA((3, chunks)),
            pltpu.SemaphoreType.DMA((2, chunks)),
            pltpu.SemaphoreType.DMA((2, chunks)),
            pltpu.SemaphoreType.DMA((2, 3, chunks)),
            pltpu.SemaphoreType.DMA((2, 3, chunks)),
        ],
        compiler_params=pltpu.CompilerParams(
            collective_id=0, has_side_effects=True, vmem_limit_bytes=40 * 1024 * 1024),
        cost_estimate=pl.CostEstimate(
            flops=4 * 9 * tokens * tokens * features, bytes_accessed=8 * tokens * features,
            transcendentals=9 * tokens * tokens * features // HDIM),
        name="neighbourhood",
    )(tissue_map, query_states, key_states, value_states)


def solution(mesh):
    return jax.shard_map(
        functools.partial(on_device, mesh.shape["row"], mesh.shape["col"]),
        mesh=mesh,
        in_specs=(
            P("row", "col", None, None),
            P("row", "col", None, None),
            P("row", "col", None, None),
            P(),
        ),
        out_specs=P("row", "col", None, None),
        check_vma=False,
    )
```

```python
import functools

import jax
import jax.numpy as jnp
from jax import lax
from jax.experimental import pallas as pl
from jax.experimental.pallas import tpu as pltpu
from jax.sharding import PartitionSpec as P

HDIM = 64
LANES = 128
MESH = pl.DeviceIdType.MESH
LAG = 3
ROW_DEPTH = 2
COL_DEPTH = 3


def kernel(rows, cols, tissue_hbm, q_hbm, k_hbm, v_hbm, out_ref, kv, qv, bias, tissue, local_sem,
           tissue_sem, row_send, row_recv, col_send, col_recv):
    chunks, _, _, tokens, _ = kv.shape
    r, c = lax.axis_index("row"), lax.axis_index("col")
    ring = rows == 4
    has_up, has_down = r > 0, r < rows - 1
    has_left, has_right = c > 0, c < cols - 1
    slot = lambda a, b: (a + 1) * 3 + b + 1
    part = lambda i, s: kv.at[i, :, s]

    def lanes(i):
        return pl.ds(pl.multiple_of(i * LANES, LANES), LANES)

    def local_copies(i):
        return [
            pltpu.make_async_copy(k_hbm.at[0, 0, :, lanes(i)], kv.at[i, 0, 4], local_sem.at[0, i]),
            pltpu.make_async_copy(v_hbm.at[0, 0, :, lanes(i)], kv.at[i, 1, 4], local_sem.at[1, i]),
            pltpu.make_async_copy(q_hbm.at[0, 0, :, lanes(i)], qv.at[i], local_sem.at[2, i]),
        ]

    tissue_copy = pltpu.make_async_copy(tissue_hbm, tissue, tissue_sem)
    tissue_copy.start()

    if ring:
        near = 1 - 2 * lax.rem(r, 2)
        outer = jnp.logical_or(r == 0, r == 3)
        inner = jnp.logical_and(r > 0, r < 3)
        across = jnp.where(r < 2, r + 2, r - 2)
        channels = [
            (None, near, None, r + near, slot(0, 0), slot(-near, 0)),
            (inner, -near, outer, across, slot(near, 0), slot(-near, 0)),
        ]
        greet = [(None, r + near), (None, across)]
    else:
        channels = [
            (has_up, -1, has_down, r + 1, slot(0, 0), slot(-1, 0)),
            (has_down, 1, has_up, r - 1, slot(0, 0), slot(1, 0)),
        ]
        greet = [(has_up, r - 1), (has_down, r + 1)]

    def when(cond, f):
        if cond is None:
            f()
        else:
            pl.when(cond)(f)

    barrier = pltpu.get_barrier_semaphore()
    count = 0
    for cond, other in greet:
        when(cond, lambda other=other: pl.semaphore_signal(
            barrier, inc=1, device_id=(other, c), device_id_type=MESH))
        count = count + (1 if cond is None else cond.astype(jnp.int32))
    for cond, other in ((has_left, c - 1), (has_right, c + 1)):
        when(cond, lambda other=other: pl.semaphore_signal(
            barrier, inc=1, device_id=(r, other), device_id_type=MESH))
        count = count + cond.astype(jnp.int32)

    @pl.loop(0, chunks)
    def _(i):
        for copy in local_copies(i):
            copy.start()

    tissue_copy.wait()
    for a in (-1, 0, 1):
        for b in (-1, 0, 1):
            s = slot(a, b)
            if (a, b) == (0, 0):
                bias[:, s * tokens:(s + 1) * tokens] = jnp.zeros((8, tokens), jnp.float32)
                continue
            inside = jnp.logical_and(jnp.logical_and(r + a >= 0, r + a < rows),
                                     jnp.logical_and(c + b >= 0, c + b < cols))
            entry = tissue[jnp.clip(r + a, 0, rows - 1), jnp.clip(c + b, 0, cols - 1)]
            live = jnp.where(inside, entry, 0) > 0
            shift = jnp.where(live, jnp.float32(0), jnp.float32(-jnp.inf))
            bias[:, s * tokens:(s + 1) * tokens] = jnp.full((8, tokens), shift, jnp.float32)

            @pl.when(jnp.logical_not(inside))
            def _():
                @pl.loop(0, chunks)
                def _(i):
                    kv[i, :, s] = jnp.zeros((2, tokens, LANES), kv.dtype)

    pl.semaphore_wait(barrier, count)

    def row_copy(ch, i):
        _, _, _, target, source, landing = channels[ch]
        return pltpu.make_async_remote_copy(
            src_ref=part(i, source), dst_ref=part(i, landing),
            send_sem=row_send.at[ch, i], recv_sem=row_recv.at[ch, i],
            device_id=(target, c), device_id_type=MESH)

    def col_copy(direction, which, i):
        a = 0 if which == 0 else channels[which - 1][1]
        b = -1 if direction == 0 else 1
        return pltpu.make_async_remote_copy(
            src_ref=part(i, slot(a, 0)), dst_ref=part(i, slot(a, b)),
            send_sem=col_send.at[direction, which, i], recv_sem=col_recv.at[direction, which, i],
            device_id=(r, c - b), device_id_type=MESH)

    def row_starts(i):
        for ch in (0, 1):
            when(channels[ch][2], lambda: row_copy(ch, i).start())

    def col_sends(which, i):
        when(has_right, lambda: col_copy(0, which, i).start())
        when(has_left, lambda: col_copy(1, which, i).start())

    depth = ROW_DEPTH if ring else chunks

    @pl.loop(0, chunks)
    def _(i):
        for copy in local_copies(i):
            copy.wait()

        @pl.when(i < depth)
        def _():
            if ring:
                row_copy(0, i).start()
            else:
                row_starts(i)

        pl.when(i < COL_DEPTH)(lambda: col_sends(0, i))

    def first(i):
        def step():
            row_copy(0, i).wait_recv()
            if ring:
                when(channels[1][2], lambda: row_copy(1, i).start())
                pl.when(i + depth < chunks)(lambda: row_copy(0, i + depth).start())
            col_sends(1, i)
        when(channels[0][0], step)
        pl.when(i + COL_DEPTH < chunks)(lambda: col_sends(0, i + COL_DEPTH))

    def second(i):
        def step():
            row_copy(1, i).wait_recv()
            col_sends(2, i)
        when(channels[1][0], step)

    def forward(i):
        first(i)
        pl.when(i > 0)(lambda: second(i - 1))

    own = tissue[r, c].astype(jnp.float32)
    low = lax.broadcasted_iota(jnp.int32, (tokens, LANES), 1) < HDIM

    def compute(i):
        for direction, cond in ((0, has_left), (1, has_right)):
            for which in (0, 1, 2):
                there = cond
                if which and channels[which - 1][0] is not None:
                    there = jnp.logical_and(cond, channels[which - 1][0])
                when(there, lambda: col_copy(direction, which, i).wait_recv())
        q = qv[i] * jnp.bfloat16(HDIM ** -0.5)
        zero = jnp.zeros_like(q)
        pair = jnp.concatenate([jnp.where(low, q, zero), jnp.where(low, zero, q)], axis=0)
        keys = kv[i, 0].reshape(9 * tokens, LANES)
        values = kv[i, 1].reshape(9 * tokens, LANES)
        scores = lax.dot_general(pair, keys, (((1,), (1,)), ((), ())), preferred_element_type=jnp.float32)
        scores = scores + bias[0:1, :]
        weights = jnp.exp(scores - jnp.max(scores, axis=1, keepdims=True))
        totals = jnp.sum(weights, axis=1, keepdims=True)
        mixed = jnp.dot(weights.astype(jnp.bfloat16), values, preferred_element_type=jnp.float32)
        mixed = mixed / totals * own
        out_ref[0, 0, :, lanes(i)] = jnp.where(low, mixed[:tokens], mixed[tokens:]).astype(out_ref.dtype)

    @pl.loop(0, LAG)
    def _(i):
        forward(i)

    @pl.loop(LAG, chunks)
    def _(i):
        forward(i)
        compute(i - LAG)

    second(chunks - 1)

    @pl.loop(chunks - LAG, chunks)
    def _(i):
        compute(i)

    @pl.loop(0, chunks)
    def _(i):
        for ch in (0, 1):
            when(channels[ch][2], lambda: row_copy(ch, i).wait_send())
        for which in (0, 1, 2):
            for direction, cond in ((0, has_right), (1, has_left)):
                there = cond
                if which and channels[which - 1][0] is not None:
                    there = jnp.logical_and(cond, channels[which - 1][0])
                when(there, lambda: col_copy(direction, which, i).wait_send())


def on_device(rows, cols, query_states, key_states, value_states, tissue_map):
    _, _, tokens, features = query_states.shape
    chunks = features // LANES
    in_hbm = pl.BlockSpec(memory_space=pltpu.HBM)
    return pl.pallas_call(
        functools.partial(kernel, rows, cols),
        out_shape=jax.ShapeDtypeStruct(query_states.shape, jnp.bfloat16),
        in_specs=[in_hbm] * 4,
        out_specs=pl.BlockSpec(memory_space=pltpu.VMEM),
        scratch_shapes=[
            pltpu.VMEM((chunks, 2, 9, tokens, LANES), jnp.bfloat16),
            pltpu.VMEM((chunks, tokens, LANES), jnp.bfloat16),
            pltpu.VMEM((8, 9 * tokens), jnp.float32),
            pltpu.SMEM(tissue_map.shape, jnp.int32),
            pltpu.SemaphoreType.DMA((3, chunks)),
            pltpu.SemaphoreType.DMA,
            pltpu.SemaphoreType.DMA((2, chunks)),
            pltpu.SemaphoreType.DMA((2, chunks)),
            pltpu.SemaphoreType.DMA((2, 3, chunks)),
            pltpu.SemaphoreType.DMA((2, 3, chunks)),
        ],
        compiler_params=pltpu.CompilerParams(
            collective_id=0, has_side_effects=True, vmem_limit_bytes=63 * 1024 * 1024),
        cost_estimate=pl.CostEstimate(
            flops=4 * 9 * tokens * tokens * features, bytes_accessed=8 * tokens * features,
            transcendentals=9 * tokens * tokens * features // HDIM),
        name="neighbourhood",
    )(tissue_map, query_states, key_states, value_states)


def solution(mesh):
    return jax.shard_map(
        functools.partial(on_device, mesh.shape["row"], mesh.shape["col"]),
        mesh=mesh,
        in_specs=(
            P("row", "col", None, None),
            P("row", "col", None, None),
            P("row", "col", None, None),
            P(),
        ),
        out_specs=P("row", "col", None, None),
        check_vma=False,
    )
```

```python
import functools

import jax
import jax.numpy as jnp
from jax import lax
from jax.experimental import pallas as pl
from jax.experimental.pallas import tpu as pltpu
from jax.sharding import PartitionSpec as P

HDIM = 64
LANES = 128
MESH = pl.DeviceIdType.MESH
LAG = 3
ROW_DEPTH = 2
COL_DEPTH = 3


def kernel(rows, cols, tissue_hbm, q_hbm, k_hbm, v_hbm, out_ref, kv, raw, qt, tissue, local_sem,
           tissue_sem, row_send, row_recv, col_send, col_recv):
    chunks, _, _, tokens, _ = kv.shape
    r, c = lax.axis_index("row"), lax.axis_index("col")
    ring = rows == 4
    has_up, has_down = r > 0, r < rows - 1
    has_left, has_right = c > 0, c < cols - 1
    slot = lambda a, b: (a + 1) * 3 + b + 1
    part = lambda i, s: kv.at[i, :, s]

    def lanes(i):
        return pl.ds(pl.multiple_of(i * LANES, LANES), LANES)

    def local_copies(i):
        return [
            pltpu.make_async_copy(k_hbm.at[0, 0, :, lanes(i)], kv.at[i, 0, 4], local_sem.at[0, i]),
            pltpu.make_async_copy(v_hbm.at[0, 0, :, lanes(i)], raw.at[1, i], local_sem.at[1, i]),
            pltpu.make_async_copy(q_hbm.at[0, 0, :, lanes(i)], raw.at[0, i], local_sem.at[2, i]),
        ]

    tissue_copy = pltpu.make_async_copy(tissue_hbm, tissue, tissue_sem)
    tissue_copy.start()

    if ring:
        near = 1 - 2 * lax.rem(r, 2)
        outer = jnp.logical_or(r == 0, r == 3)
        inner = jnp.logical_and(r > 0, r < 3)
        across = jnp.where(r < 2, r + 2, r - 2)
        channels = [
            (None, near, None, r + near, slot(0, 0), slot(-near, 0)),
            (inner, -near, outer, across, slot(near, 0), slot(-near, 0)),
        ]
        greet = [(None, r + near), (None, across)]
    else:
        channels = [
            (has_up, -1, has_down, r + 1, slot(0, 0), slot(-1, 0)),
            (has_down, 1, has_up, r - 1, slot(0, 0), slot(1, 0)),
        ]
        greet = [(has_up, r - 1), (has_down, r + 1)]

    def when(cond, f):
        if cond is None:
            f()
        else:
            pl.when(cond)(f)

    barrier = pltpu.get_barrier_semaphore()
    count = 0
    for cond, other in greet:
        when(cond, lambda other=other: pl.semaphore_signal(
            barrier, inc=1, device_id=(other, c), device_id_type=MESH))
        count = count + (1 if cond is None else cond.astype(jnp.int32))
    for cond, other in ((has_left, c - 1), (has_right, c + 1)):
        when(cond, lambda other=other: pl.semaphore_signal(
            barrier, inc=1, device_id=(r, other), device_id_type=MESH))
        count = count + cond.astype(jnp.int32)

    @pl.loop(0, chunks)
    def _(i):
        for copy in local_copies(i):
            copy.start()

    tissue_copy.wait()
    shifts = []
    for a in (-1, 0, 1):
        for b in (-1, 0, 1):
            s = slot(a, b)
            if (a, b) == (0, 0):
                shifts.append(None)
                continue
            inside = jnp.logical_and(jnp.logical_and(r + a >= 0, r + a < rows),
                                     jnp.logical_and(c + b >= 0, c + b < cols))
            entry = tissue[jnp.clip(r + a, 0, rows - 1), jnp.clip(c + b, 0, cols - 1)]
            live = jnp.where(inside, entry, 0) > 0
            shifts.append(jnp.where(live, jnp.float32(0), jnp.float32(-jnp.inf)))

            @pl.when(jnp.logical_not(inside))
            def _():
                @pl.loop(0, chunks)
                def _(i):
                    kv[i, :, s] = jnp.zeros((2, tokens, LANES), kv.dtype)

    low = lax.broadcasted_iota(jnp.int32, (LANES, tokens), 0) < HDIM

    @pl.loop(0, chunks)
    def _(i):
        for copy in local_copies(i):
            copy.wait()
        kv[i, 1, 4] = raw[1, i].T
        q = (raw[0, i] * jnp.bfloat16(HDIM ** -0.5)).T
        zero = jnp.zeros_like(q)
        qt[i, :, :tokens] = jnp.where(low, q, zero)
        qt[i, :, tokens:] = jnp.where(low, zero, q)

    pl.semaphore_wait(barrier, count)

    def row_copy(ch, i):
        _, _, _, target, source, landing = channels[ch]
        return pltpu.make_async_remote_copy(
            src_ref=part(i, source), dst_ref=part(i, landing),
            send_sem=row_send.at[ch, i], recv_sem=row_recv.at[ch, i],
            device_id=(target, c), device_id_type=MESH)

    def col_copy(direction, which, i):
        a = 0 if which == 0 else channels[which - 1][1]
        b = -1 if direction == 0 else 1
        return pltpu.make_async_remote_copy(
            src_ref=part(i, slot(a, 0)), dst_ref=part(i, slot(a, b)),
            send_sem=col_send.at[direction, which, i], recv_sem=col_recv.at[direction, which, i],
            device_id=(r, c - b), device_id_type=MESH)

    def row_starts(i):
        for ch in (0, 1):
            when(channels[ch][2], lambda: row_copy(ch, i).start())

    def col_sends(which, i):
        when(has_right, lambda: col_copy(0, which, i).start())
        when(has_left, lambda: col_copy(1, which, i).start())

    depth = ROW_DEPTH if ring else chunks

    @pl.loop(0, chunks)
    def _(i):
        @pl.when(i < depth)
        def _():
            if ring:
                row_copy(0, i).start()
            else:
                row_starts(i)

        pl.when(i < COL_DEPTH)(lambda: col_sends(0, i))

    def first(i):
        def step():
            row_copy(0, i).wait_recv()
            if ring:
                when(channels[1][2], lambda: row_copy(1, i).start())
                pl.when(i + depth < chunks)(lambda: row_copy(0, i + depth).start())
            col_sends(1, i)
        when(channels[0][0], step)
        pl.when(i + COL_DEPTH < chunks)(lambda: col_sends(0, i + COL_DEPTH))

    def second(i):
        def step():
            row_copy(1, i).wait_recv()
            col_sends(2, i)
        when(channels[1][0], step)

    def forward(i):
        first(i)
        pl.when(i > 0)(lambda: second(i - 1))

    own = tissue[r, c].astype(jnp.float32)
    own = tissue[r, c].astype(jnp.float32)

    def compute(i):
        for direction, cond in ((0, has_left), (1, has_right)):
            for which in (0, 1, 2):
                there = cond
                if which and channels[which - 1][0] is not None:
                    there = jnp.logical_and(cond, channels[which - 1][0])
                when(there, lambda: col_copy(direction, which, i).wait_recv())
        queries = qt[i]
        scores = []
        for s, shift in enumerate(shifts):
            tile = jnp.dot(kv[i, 0, s], queries, preferred_element_type=jnp.float32)
            scores.append(tile if shift is None else tile + shift)
        top = jnp.max(functools.reduce(jnp.maximum, scores), axis=0, keepdims=True)
        weights = [jnp.exp(tile - top) for tile in scores]
        totals = jnp.sum(functools.reduce(jnp.add, weights), axis=0, keepdims=True)
        rounded = jnp.concatenate([tile.astype(jnp.bfloat16) for tile in weights], axis=0)
        values = jnp.concatenate([kv[i, 1, s] for s in range(9)], axis=1)
        mixed = jnp.dot(values, rounded, preferred_element_type=jnp.float32)
        mixed = mixed / totals * own
        mixed = jnp.concatenate([mixed[:HDIM, :tokens], mixed[HDIM:, tokens:]], axis=0)
        out_ref[0, 0, :, lanes(i)] = mixed.T.astype(out_ref.dtype)

    @pl.loop(0, LAG)
    def _(i):
        forward(i)

    @pl.loop(LAG, chunks)
    def _(i):
        forward(i)
        compute(i - LAG)

    second(chunks - 1)

    @pl.loop(chunks - LAG, chunks)
    def _(i):
        compute(i)

    @pl.loop(0, chunks)
    def _(i):
        for ch in (0, 1):
            when(channels[ch][2], lambda: row_copy(ch, i).wait_send())
        for which in (0, 1, 2):
            for direction, cond in ((0, has_right), (1, has_left)):
                there = cond
                if which and channels[which - 1][0] is not None:
                    there = jnp.logical_and(cond, channels[which - 1][0])
                when(there, lambda: col_copy(direction, which, i).wait_send())


def on_device(rows, cols, query_states, key_states, value_states, tissue_map):
    _, _, tokens, features = query_states.shape
    chunks = features // LANES
    in_hbm = pl.BlockSpec(memory_space=pltpu.HBM)
    return pl.pallas_call(
        functools.partial(kernel, rows, cols),
        out_shape=pltpu.VMEM(query_states.shape, jnp.bfloat16),
        in_specs=[in_hbm] * 4,
        out_specs=pl.BlockSpec(memory_space=pltpu.VMEM),
        scratch_shapes=[
            pltpu.VMEM((chunks, 2, 9, tokens, LANES), jnp.bfloat16),
            pltpu.VMEM((2, chunks, tokens, LANES), jnp.bfloat16),
            pltpu.VMEM((chunks, LANES, 2 * tokens), jnp.bfloat16),
            pltpu.SMEM(tissue_map.shape, jnp.int32),
            pltpu.SemaphoreType.DMA((3, chunks)),
            pltpu.SemaphoreType.DMA,
            pltpu.SemaphoreType.DMA((2, chunks)),
            pltpu.SemaphoreType.DMA((2, chunks)),
            pltpu.SemaphoreType.DMA((2, 3, chunks)),
            pltpu.SemaphoreType.DMA((2, 3, chunks)),
        ],
        compiler_params=pltpu.CompilerParams(
            collective_id=0, has_side_effects=True, vmem_limit_bytes=60 * 1024 * 1024),
        cost_estimate=pl.CostEstimate(
            flops=4 * 9 * tokens * tokens * features, bytes_accessed=8 * tokens * features,
            transcendentals=9 * tokens * tokens * features // HDIM),
        name="neighbourhood",
    )(tissue_map, query_states, key_states, value_states)


def solution(mesh):
    return jax.shard_map(
        functools.partial(on_device, mesh.shape["row"], mesh.shape["col"]),
        mesh=mesh,
        in_specs=(
            P("row", "col", None, None),
            P("row", "col", None, None),
            P("row", "col", None, None),
            P(),
        ),
        out_specs=P("row", "col", None, None),
        check_vma=False,
    )
```

```python
import functools

import jax
import jax.numpy as jnp
from jax import lax
from jax.experimental import pallas as pl
from jax.experimental.pallas import tpu as pltpu
from jax.sharding import PartitionSpec as P

HDIM = 64
LANES = 128
MESH = pl.DeviceIdType.MESH
LAG = 3
ROW_DEPTH = 2
COL_DEPTH = 3
NEAR = (4, 6)
FAR = (2, 4)


def kernel(rows, cols, tissue_hbm, q_hbm, k_hbm, v_hbm, out_ref, kv, raw, qt, tissue, local_sem,
           tissue_sem, row_send, row_recv, col_send, col_recv, cross_send, cross_recv):
    chunks, _, _, tokens, _ = kv.shape
    r, c = lax.axis_index("row"), lax.axis_index("col")
    ring = rows == 4
    has_up, has_down = r > 0, r < rows - 1
    has_left, has_right = c > 0, c < cols - 1
    slot = lambda a, b: (a + 1) * 3 + b + 1
    part = lambda i, s: kv.at[i, :, s]

    def lanes(i):
        return pl.ds(pl.multiple_of(i * LANES, LANES), LANES)

    def local_copies(i):
        return [
            pltpu.make_async_copy(k_hbm.at[0, 0, :, lanes(i)], kv.at[i, 0, 4], local_sem.at[0, i]),
            pltpu.make_async_copy(v_hbm.at[0, 0, :, lanes(i)], raw.at[1, i], local_sem.at[1, i]),
            pltpu.make_async_copy(q_hbm.at[0, 0, :, lanes(i)], raw.at[0, i], local_sem.at[2, i]),
        ]

    tissue_copy = pltpu.make_async_copy(tissue_hbm, tissue, tissue_sem)
    tissue_copy.start()

    if ring:
        near = 1 - 2 * lax.rem(r, 2)
        outer = jnp.logical_or(r == 0, r == 3)
        inner = jnp.logical_and(r > 0, r < 3)
        across = jnp.where(r < 2, r + 2, r - 2)
        channels = [
            (None, near, None, r + near, slot(0, 0), slot(-near, 0)),
            (inner, -near, outer, across, slot(near, 0), slot(-near, 0)),
        ]
        greet = [(None, r + near), (None, across)]
    else:
        channels = [
            (has_up, -1, has_down, r + 1, slot(0, 0), slot(-1, 0)),
            (has_down, 1, has_up, r - 1, slot(0, 0), slot(1, 0)),
        ]
        greet = [(has_up, r - 1), (has_down, r + 1)]

    def when(cond, f):
        if cond is None:
            f()
        else:
            pl.when(cond)(f)

    barrier = pltpu.get_barrier_semaphore()
    count = 0
    for cond, other in greet:
        when(cond, lambda other=other: pl.semaphore_signal(
            barrier, inc=1, device_id=(other, c), device_id_type=MESH))
        count = count + (1 if cond is None else cond.astype(jnp.int32))
    for cond, other in ((has_left, c - 1), (has_right, c + 1)):
        when(cond, lambda other=other: pl.semaphore_signal(
            barrier, inc=1, device_id=(r, other), device_id_type=MESH))
        count = count + cond.astype(jnp.int32)

    @pl.loop(0, chunks)
    def _(i):
        for copy in local_copies(i):
            copy.start()

    tissue_copy.wait()
    shifts = []
    for a in (-1, 0, 1):
        for b in (-1, 0, 1):
            s = slot(a, b)
            if (a, b) == (0, 0):
                shifts.append(None)
                continue
            inside = jnp.logical_and(jnp.logical_and(r + a >= 0, r + a < rows),
                                     jnp.logical_and(c + b >= 0, c + b < cols))
            entry = tissue[jnp.clip(r + a, 0, rows - 1), jnp.clip(c + b, 0, cols - 1)]
            live = jnp.where(inside, entry, 0) > 0
            shifts.append(jnp.where(live, jnp.float32(0), jnp.float32(-jnp.inf)))

            @pl.when(jnp.logical_not(inside))
            def _():
                @pl.loop(0, chunks)
                def _(i):
                    kv[i, :, s] = jnp.zeros((2, tokens, LANES), kv.dtype)

    low = lax.broadcasted_iota(jnp.int32, (LANES, tokens), 0) < HDIM

    @pl.loop(0, chunks)
    def _(i):
        for copy in local_copies(i):
            copy.wait()
        kv[i, 1, 4] = raw[1, i].T
        q = (raw[0, i] * jnp.bfloat16(HDIM ** -0.5)).T
        zero = jnp.zeros_like(q)
        qt[i, :, :tokens] = jnp.where(low, q, zero)
        qt[i, :, tokens:] = jnp.where(low, zero, q)

    pl.semaphore_wait(barrier, count)

    def row_copy(ch, i):
        _, _, _, target, source, landing = channels[ch]
        return pltpu.make_async_remote_copy(
            src_ref=part(i, source), dst_ref=part(i, landing),
            send_sem=row_send.at[ch, i], recv_sem=row_recv.at[ch, i],
            device_id=(target, c), device_id_type=MESH)

    def col_copy(direction, which, i):
        a = 0 if which == 0 else channels[which - 1][1]
        b = -1 if direction == 0 else 1
        return pltpu.make_async_remote_copy(
            src_ref=part(i, slot(a, 0)), dst_ref=part(i, slot(a, b)),
            send_sem=col_send.at[direction, which, i], recv_sem=col_recv.at[direction, which, i],
            device_id=(r, c - b), device_id_type=MESH)

    odd = lax.rem(c, 2)
    side = 2 * odd - 1
    has_side = jnp.logical_and(c + side >= 0, c + side < cols)
    spans = (NEAR, FAR) if ring else ((0, 0), (0, 0))

    def moved(kind, i):
        return jnp.logical_and(i >= spans[kind][0], i < spans[kind][1])

    def cross_copy(kind, i):
        source, target = (slot(0, side), r + near) if kind == 0 else (slot(near, side), across)
        return pltpu.make_async_remote_copy(
            src_ref=part(i, source), dst_ref=part(i, slot(-near, side)),
            send_sem=cross_send.at[kind, i], recv_sem=cross_recv.at[kind, i],
            device_id=(target, c), device_id_type=MESH)

    def by_column(direction, which, i, sending):
        if which == 0 or not ring:
            return True
        at_side = odd == (1 - direction if sending else direction)
        return jnp.logical_not(jnp.logical_and(at_side, moved(which - 1, i)))

    def row_starts(i):
        for ch in (0, 1):
            when(channels[ch][2], lambda: row_copy(ch, i).start())

    def col_sends(which, i):
        for direction, cond in ((0, has_right), (1, has_left)):
            there = jnp.logical_and(cond, by_column(direction, which, i, True))
            when(there, lambda: col_copy(direction, which, i).start())

    depth = ROW_DEPTH if ring else chunks

    @pl.loop(0, chunks)
    def _(i):
        @pl.when(i < depth)
        def _():
            if ring:
                row_copy(0, i).start()
            else:
                row_starts(i)

        pl.when(i < COL_DEPTH)(lambda: col_sends(0, i))

    def first(i):
        def step():
            row_copy(0, i).wait_recv()
            if ring:
                when(channels[1][2], lambda: row_copy(1, i).start())
                pl.when(i + depth < chunks)(lambda: row_copy(0, i + depth).start())
            col_sends(1, i)
        when(channels[0][0], step)
        pl.when(i + COL_DEPTH < chunks)(lambda: col_sends(0, i + COL_DEPTH))

    def second(i):
        def step():
            row_copy(1, i).wait_recv()
            col_sends(2, i)
        when(channels[1][0], step)

    def cross(kind, i):
        def step():
            for d in (0, 1):
                pl.when(odd == d)(lambda: col_copy(d, kind, i).wait_recv())
            cross_copy(kind, i).start()
        cond = has_side if kind == 0 else jnp.logical_and(has_side, outer)
        pl.when(jnp.logical_and(cond, moved(kind, i)))(step)

    def forward(i):
        first(i)
        pl.when(i > 0)(lambda: second(i - 1))
        if ring:
            cross(0, i)
            pl.when(i >= 2)(lambda: cross(1, i - 2))

    own = tissue[r, c].astype(jnp.float32)
    own = tissue[r, c].astype(jnp.float32)

    def compute(i):
        for direction, cond in ((0, has_left), (1, has_right)):
            for which in (0, 1, 2):
                there = cond
                if which and channels[which - 1][0] is not None:
                    there = jnp.logical_and(cond, channels[which - 1][0])
                there = jnp.logical_and(there, by_column(direction, which, i, False))
                if ring and which < 2:
                    passed = jnp.logical_and(odd == direction, moved(which, i))
                    if which == 1:
                        passed = jnp.logical_and(passed, outer)
                    there = jnp.logical_and(there, jnp.logical_not(passed))
                when(there, lambda: col_copy(direction, which, i).wait_recv())
        if ring:
            pl.when(jnp.logical_and(has_side, moved(0, i)))(lambda: cross_copy(0, i).wait_recv())
            pl.when(jnp.logical_and(jnp.logical_and(has_side, inner), moved(1, i)))(
                lambda: cross_copy(1, i).wait_recv())
        queries = qt[i]
        scores = []
        for s, shift in enumerate(shifts):
            tile = jnp.dot(kv[i, 0, s], queries, preferred_element_type=jnp.float32)
            scores.append(tile if shift is None else tile + shift)
        top = jnp.max(functools.reduce(jnp.maximum, scores), axis=0, keepdims=True)
        weights = [jnp.exp(tile - top) for tile in scores]
        totals = jnp.sum(functools.reduce(jnp.add, weights), axis=0, keepdims=True)
        rounded = jnp.concatenate([tile.astype(jnp.bfloat16) for tile in weights], axis=0)
        values = jnp.concatenate([kv[i, 1, s] for s in range(9)], axis=1)
        mixed = jnp.dot(values, rounded, preferred_element_type=jnp.float32)
        mixed = mixed / totals * own
        mixed = jnp.concatenate([mixed[:HDIM, :tokens], mixed[HDIM:, tokens:]], axis=0)
        out_ref[0, 0, :, lanes(i)] = mixed.T.astype(out_ref.dtype)

    @pl.loop(0, LAG)
    def _(i):
        forward(i)

    @pl.loop(LAG, chunks)
    def _(i):
        forward(i)
        compute(i - LAG)

    second(chunks - 1)

    @pl.loop(chunks - LAG, chunks)
    def _(i):
        compute(i)

    @pl.loop(0, chunks)
    def _(i):
        for ch in (0, 1):
            when(channels[ch][2], lambda: row_copy(ch, i).wait_send())
        for which in (0, 1, 2):
            for direction, cond in ((0, has_right), (1, has_left)):
                there = cond
                if which and channels[which - 1][0] is not None:
                    there = jnp.logical_and(cond, channels[which - 1][0])
                there = jnp.logical_and(there, by_column(direction, which, i, True))
                when(there, lambda: col_copy(direction, which, i).wait_send())
        if ring:
            pl.when(jnp.logical_and(has_side, moved(0, i)))(lambda: cross_copy(0, i).wait_send())
            pl.when(jnp.logical_and(jnp.logical_and(has_side, outer), moved(1, i)))(
                lambda: cross_copy(1, i).wait_send())


def on_device(rows, cols, query_states, key_states, value_states, tissue_map):
    _, _, tokens, features = query_states.shape
    chunks = features // LANES
    in_hbm = pl.BlockSpec(memory_space=pltpu.HBM)
    return pl.pallas_call(
        functools.partial(kernel, rows, cols),
        out_shape=pltpu.VMEM(query_states.shape, jnp.bfloat16),
        in_specs=[in_hbm] * 4,
        out_specs=pl.BlockSpec(memory_space=pltpu.VMEM),
        scratch_shapes=[
            pltpu.VMEM((chunks, 2, 9, tokens, LANES), jnp.bfloat16),
            pltpu.VMEM((2, chunks, tokens, LANES), jnp.bfloat16),
            pltpu.VMEM((chunks, LANES, 2 * tokens), jnp.bfloat16),
            pltpu.SMEM(tissue_map.shape, jnp.int32),
            pltpu.SemaphoreType.DMA((3, chunks)),
            pltpu.SemaphoreType.DMA,
            pltpu.SemaphoreType.DMA((2, chunks)),
            pltpu.SemaphoreType.DMA((2, chunks)),
            pltpu.SemaphoreType.DMA((2, 3, chunks)),
            pltpu.SemaphoreType.DMA((2, 3, chunks)),
            pltpu.SemaphoreType.DMA((2, chunks)),
            pltpu.SemaphoreType.DMA((2, chunks)),
        ],
        compiler_params=pltpu.CompilerParams(
            collective_id=0, has_side_effects=True, vmem_limit_bytes=60 * 1024 * 1024),
        cost_estimate=pl.CostEstimate(
            flops=4 * 9 * tokens * tokens * features, bytes_accessed=8 * tokens * features,
            transcendentals=9 * tokens * tokens * features // HDIM),
        name="neighbourhood",
    )(tissue_map, query_states, key_states, value_states)


def solution(mesh):
    return jax.shard_map(
        functools.partial(on_device, mesh.shape["row"], mesh.shape["col"]),
        mesh=mesh,
        in_specs=(
            P("row", "col", None, None),
            P("row", "col", None, None),
            P("row", "col", None, None),
            P(),
        ),
        out_specs=P("row", "col", None, None),
        check_vma=False,
    )
```

```python
import functools

import jax
import jax.numpy as jnp
from jax import lax
from jax.experimental import pallas as pl
from jax.experimental.pallas import tpu as pltpu
from jax.sharding import PartitionSpec as P

HDIM = 64
LANES = 128
MESH = pl.DeviceIdType.MESH
LAG = 4
ROW_DEPTH = 3
COL_DEPTH = 2


def kernel(rows, cols, tissue_hbm, q_hbm, k_hbm, v_hbm, out_ref, kv, raw, qt, tissue, local_sem,
           tissue_sem, row_send, row_recv, col_send, col_recv):
    chunks, _, _, tokens, _ = kv.shape
    r, c = lax.axis_index("row"), lax.axis_index("col")
    ring = rows == 4
    has_up, has_down = r > 0, r < rows - 1
    has_left, has_right = c > 0, c < cols - 1
    slot = lambda a, b: (a + 1) * 3 + b + 1
    part = lambda i, s: kv.at[i, :, s]

    def lanes(i):
        return pl.ds(pl.multiple_of(i * LANES, LANES), LANES)

    def local_copies(i):
        return [
            pltpu.make_async_copy(k_hbm.at[0, 0, :, lanes(i)], kv.at[i, 0, 4], local_sem.at[0, i]),
            pltpu.make_async_copy(v_hbm.at[0, 0, :, lanes(i)], raw.at[1, i], local_sem.at[1, i]),
            pltpu.make_async_copy(q_hbm.at[0, 0, :, lanes(i)], raw.at[0, i], local_sem.at[2, i]),
        ]

    tissue_copy = pltpu.make_async_copy(tissue_hbm, tissue, tissue_sem)
    tissue_copy.start()

    if ring:
        near = 1 - 2 * lax.rem(r, 2)
        outer = jnp.logical_or(r == 0, r == 3)
        inner = jnp.logical_and(r > 0, r < 3)
        across = jnp.where(r < 2, r + 2, r - 2)
        channels = [
            (None, near, None, r + near, slot(0, 0), slot(-near, 0)),
            (inner, -near, outer, across, slot(near, 0), slot(-near, 0)),
        ]
        greet = [(None, r + near), (None, across)]
    else:
        channels = [
            (has_up, -1, has_down, r + 1, slot(0, 0), slot(-1, 0)),
            (has_down, 1, has_up, r - 1, slot(0, 0), slot(1, 0)),
        ]
        greet = [(has_up, r - 1), (has_down, r + 1)]

    def when(cond, f):
        if cond is None:
            f()
        else:
            pl.when(cond)(f)

    barrier = pltpu.get_barrier_semaphore()
    count = 0
    for cond, other in greet:
        when(cond, lambda other=other: pl.semaphore_signal(
            barrier, inc=1, device_id=(other, c), device_id_type=MESH))
        count = count + (1 if cond is None else cond.astype(jnp.int32))
    for cond, other in ((has_left, c - 1), (has_right, c + 1)):
        when(cond, lambda other=other: pl.semaphore_signal(
            barrier, inc=1, device_id=(r, other), device_id_type=MESH))
        count = count + cond.astype(jnp.int32)

    @pl.loop(0, chunks)
    def _(i):
        for copy in local_copies(i):
            copy.start()

    tissue_copy.wait()
    shifts = []
    for a in (-1, 0, 1):
        for b in (-1, 0, 1):
            s = slot(a, b)
            if (a, b) == (0, 0):
                shifts.append(None)
                continue
            inside = jnp.logical_and(jnp.logical_and(r + a >= 0, r + a < rows),
                                     jnp.logical_and(c + b >= 0, c + b < cols))
            entry = tissue[jnp.clip(r + a, 0, rows - 1), jnp.clip(c + b, 0, cols - 1)]
            live = jnp.where(inside, entry, 0) > 0
            shifts.append(jnp.where(live, jnp.float32(0), jnp.float32(-jnp.inf)))

            @pl.when(jnp.logical_not(inside))
            def _():
                @pl.loop(0, chunks)
                def _(i):
                    kv[i, :, s] = jnp.zeros((2, tokens, LANES), kv.dtype)

    low = lax.broadcasted_iota(jnp.int32, (LANES, tokens), 0) < HDIM

    @pl.loop(0, chunks)
    def _(i):
        for copy in local_copies(i):
            copy.wait()
        kv[i, 1, 4] = raw[1, i].T
        q = (raw[0, i] * jnp.bfloat16(HDIM ** -0.5)).T
        zero = jnp.zeros_like(q)
        qt[i, :, :tokens] = jnp.where(low, q, zero)
        qt[i, :, tokens:] = jnp.where(low, zero, q)

    pl.semaphore_wait(barrier, count)

    def row_copy(ch, i):
        _, _, _, target, source, landing = channels[ch]
        return pltpu.make_async_remote_copy(
            src_ref=part(i, source), dst_ref=part(i, landing),
            send_sem=row_send.at[ch, i], recv_sem=row_recv.at[ch, i],
            device_id=(target, c), device_id_type=MESH)

    def col_copy(direction, which, i):
        a = 0 if which == 0 else channels[which - 1][1]
        b = -1 if direction == 0 else 1
        return pltpu.make_async_remote_copy(
            src_ref=part(i, slot(a, 0)), dst_ref=part(i, slot(a, b)),
            send_sem=col_send.at[direction, which, i], recv_sem=col_recv.at[direction, which, i],
            device_id=(r, c - b), device_id_type=MESH)

    def row_starts(i):
        for ch in (0, 1):
            when(channels[ch][2], lambda: row_copy(ch, i).start())

    def col_sends(which, i):
        when(has_right, lambda: col_copy(0, which, i).start())
        when(has_left, lambda: col_copy(1, which, i).start())

    depth = ROW_DEPTH if ring else chunks

    @pl.loop(0, chunks)
    def _(i):
        @pl.when(i < depth)
        def _():
            if ring:
                row_copy(0, i).start()
            else:
                row_starts(i)

        pl.when(i < COL_DEPTH)(lambda: col_sends(0, i))

    def first(i):
        def step():
            row_copy(0, i).wait_recv()
            if ring:
                when(channels[1][2], lambda: row_copy(1, i).start())
                pl.when(i + depth < chunks)(lambda: row_copy(0, i + depth).start())
            col_sends(1, i)
        when(channels[0][0], step)
        pl.when(i + COL_DEPTH < chunks)(lambda: col_sends(0, i + COL_DEPTH))

    def second(i):
        def step():
            row_copy(1, i).wait_recv()
            col_sends(2, i)
        when(channels[1][0], step)

    def forward(i):
        first(i)
        pl.when(i > 0)(lambda: second(i - 1))

    own = tissue[r, c].astype(jnp.float32)
    own = tissue[r, c].astype(jnp.float32)

    def compute(i):
        for direction, cond in ((0, has_left), (1, has_right)):
            for which in (0, 1, 2):
                there = cond
                if which and channels[which - 1][0] is not None:
                    there = jnp.logical_and(cond, channels[which - 1][0])
                when(there, lambda: col_copy(direction, which, i).wait_recv())
        queries = qt[i]
        scores = []
        for s, shift in enumerate(shifts):
            tile = jnp.dot(kv[i, 0, s], queries, preferred_element_type=jnp.float32)
            scores.append(tile if shift is None else tile + shift)
        top = jnp.max(functools.reduce(jnp.maximum, scores), axis=0, keepdims=True)
        weights = [jnp.exp(tile - top) for tile in scores]
        totals = jnp.sum(functools.reduce(jnp.add, weights), axis=0, keepdims=True)
        rounded = jnp.concatenate([tile.astype(jnp.bfloat16) for tile in weights], axis=0)
        values = jnp.concatenate([kv[i, 1, s] for s in range(9)], axis=1)
        mixed = jnp.dot(values, rounded, preferred_element_type=jnp.float32)
        mixed = mixed / totals * own
        mixed = jnp.concatenate([mixed[:HDIM, :tokens], mixed[HDIM:, tokens:]], axis=0)
        out_ref[0, 0, :, lanes(i)] = mixed.T.astype(out_ref.dtype)

    @pl.loop(0, LAG)
    def _(i):
        forward(i)

    @pl.loop(LAG, chunks)
    def _(i):
        forward(i)
        compute(i - LAG)

    second(chunks - 1)

    @pl.loop(chunks - LAG, chunks)
    def _(i):
        compute(i)

    @pl.loop(0, chunks)
    def _(i):
        for ch in (0, 1):
            when(channels[ch][2], lambda: row_copy(ch, i).wait_send())
        for which in (0, 1, 2):
            for direction, cond in ((0, has_right), (1, has_left)):
                there = cond
                if which and channels[which - 1][0] is not None:
                    there = jnp.logical_and(cond, channels[which - 1][0])
                when(there, lambda: col_copy(direction, which, i).wait_send())


def on_device(rows, cols, query_states, key_states, value_states, tissue_map):
    _, _, tokens, features = query_states.shape
    chunks = features // LANES
    in_hbm = pl.BlockSpec(memory_space=pltpu.HBM)
    return pl.pallas_call(
        functools.partial(kernel, rows, cols),
        out_shape=pltpu.VMEM(query_states.shape, jnp.bfloat16),
        in_specs=[in_hbm] * 4,
        out_specs=pl.BlockSpec(memory_space=pltpu.VMEM),
        scratch_shapes=[
            pltpu.VMEM((chunks, 2, 9, tokens, LANES), jnp.bfloat16),
            pltpu.VMEM((2, chunks, tokens, LANES), jnp.bfloat16),
            pltpu.VMEM((chunks, LANES, 2 * tokens), jnp.bfloat16),
            pltpu.SMEM(tissue_map.shape, jnp.int32),
            pltpu.SemaphoreType.DMA((3, chunks)),
            pltpu.SemaphoreType.DMA,
            pltpu.SemaphoreType.DMA((2, chunks)),
            pltpu.SemaphoreType.DMA((2, chunks)),
            pltpu.SemaphoreType.DMA((2, 3, chunks)),
            pltpu.SemaphoreType.DMA((2, 3, chunks)),
        ],
        compiler_params=pltpu.CompilerParams(
            collective_id=0, has_side_effects=True, vmem_limit_bytes=60 * 1024 * 1024),
        cost_estimate=pl.CostEstimate(
            flops=4 * 9 * tokens * tokens * features, bytes_accessed=8 * tokens * features,
            transcendentals=9 * tokens * tokens * features // HDIM),
        name="neighbourhood",
    )(tissue_map, query_states, key_states, value_states)


def solution(mesh):
    return jax.shard_map(
        functools.partial(on_device, mesh.shape["row"], mesh.shape["col"]),
        mesh=mesh,
        in_specs=(
            P("row", "col", None, None),
            P("row", "col", None, None),
            P("row", "col", None, None),
            P(),
        ),
        out_specs=P("row", "col", None, None),
        check_vma=False,
    )
```

```python
import functools

import jax
import jax.numpy as jnp
from jax import lax
from jax.experimental import pallas as pl
from jax.experimental.pallas import tpu as pltpu
from jax.sharding import PartitionSpec as P

HDIM = 64
LANES = 128
MESH = pl.DeviceIdType.MESH
LAG = 4
ROW_DEPTH = 3
COL_DEPTH = 2


def kernel(rows, cols, tissue_hbm, q_hbm, k_hbm, v_hbm, out_ref, kv, raw, qt, tissue, local_sem,
           tissue_sem, row_send, row_recv, col_send, col_recv):
    chunks, _, _, tokens, _ = kv.shape
    r, c = lax.axis_index("row"), lax.axis_index("col")
    ring = rows == 4
    has_up, has_down = r > 0, r < rows - 1
    odd = lax.rem(c, 2) == 1
    has_left, has_right = c > 0, c < cols - 1
    slot = lambda a, b: (a + 1) * 3 + b + 1
    part = lambda i, s: kv.at[i, :, s]

    def lanes(i):
        return pl.ds(pl.multiple_of(i * LANES, LANES), LANES)

    def local_copies(i):
        return [
            pltpu.make_async_copy(k_hbm.at[0, 0, :, lanes(i)], kv.at[i, 0, 4], local_sem.at[0, i]),
            pltpu.make_async_copy(v_hbm.at[0, 0, :, lanes(i)], raw.at[1, i], local_sem.at[1, i]),
            pltpu.make_async_copy(q_hbm.at[0, 0, :, lanes(i)], raw.at[0, i], local_sem.at[2, i]),
        ]

    tissue_copy = pltpu.make_async_copy(tissue_hbm, tissue, tissue_sem)
    tissue_copy.start()

    if ring:
        near = 1 - 2 * lax.rem(r, 2)
        outer = jnp.logical_or(r == 0, r == 3)
        inner = jnp.logical_and(r > 0, r < 3)
        across = jnp.where(r < 2, r + 2, r - 2)
        channels = [
            (None, near, None, r + near, slot(0, 0), slot(-near, 0)),
            (inner, -near, outer, across, slot(near, 0), slot(-near, 0)),
        ]
        greet = [(None, r + near), (None, across)]
    else:
        channels = [
            (has_up, -1, has_down, r + 1, slot(0, 0), slot(-1, 0)),
            (has_down, 1, has_up, r - 1, slot(0, 0), slot(1, 0)),
        ]
        greet = [(has_up, r - 1), (has_down, r + 1)]

    def when(cond, f):
        if cond is None:
            f()
        else:
            pl.when(cond)(f)

    barrier = pltpu.get_barrier_semaphore()
    count = 0
    for cond, other in greet:
        when(cond, lambda other=other: pl.semaphore_signal(
            barrier, inc=1, device_id=(other, c), device_id_type=MESH))
        count = count + (1 if cond is None else cond.astype(jnp.int32))
    for cond, other in ((has_left, c - 1), (has_right, c + 1)):
        when(cond, lambda other=other: pl.semaphore_signal(
            barrier, inc=1, device_id=(r, other), device_id_type=MESH))
        count = count + cond.astype(jnp.int32)

    @pl.loop(0, chunks)
    def _(i):
        for copy in local_copies(i):
            copy.start()

    tissue_copy.wait()
    shifts = []
    for a in (-1, 0, 1):
        for b in (-1, 0, 1):
            s = slot(a, b)
            if (a, b) == (0, 0):
                shifts.append(None)
                continue
            inside = jnp.logical_and(jnp.logical_and(r + a >= 0, r + a < rows),
                                     jnp.logical_and(c + b >= 0, c + b < cols))
            entry = tissue[jnp.clip(r + a, 0, rows - 1), jnp.clip(c + b, 0, cols - 1)]
            live = jnp.where(inside, entry, 0) > 0
            shifts.append(jnp.where(live, jnp.float32(0), jnp.float32(-jnp.inf)))

            @pl.when(jnp.logical_not(inside))
            def _():
                @pl.loop(0, chunks)
                def _(i):
                    kv[i, :, s] = jnp.zeros((2, tokens, LANES), kv.dtype)

    low = lax.broadcasted_iota(jnp.int32, (LANES, tokens), 0) < HDIM

    @pl.loop(0, chunks)
    def _(i):
        for copy in local_copies(i):
            copy.wait()
        kv[i, 1, 4] = raw[1, i].T
        q = (raw[0, i] * jnp.bfloat16(HDIM ** -0.5)).T
        zero = jnp.zeros_like(q)
        qt[i, :, :tokens] = jnp.where(low, q, zero)
        qt[i, :, tokens:] = jnp.where(low, zero, q)

    pl.semaphore_wait(barrier, count)

    def row_copy(ch, i):
        _, _, _, target, source, landing = channels[ch]
        return pltpu.make_async_remote_copy(
            src_ref=part(i, source), dst_ref=part(i, landing),
            send_sem=row_send.at[ch, i], recv_sem=row_recv.at[ch, i],
            device_id=(target, c), device_id_type=MESH)

    def col_copy(direction, which, i):
        a = 0 if which == 0 else channels[which - 1][1]
        b = -1 if direction == 0 else 1
        return pltpu.make_async_remote_copy(
            src_ref=part(i, slot(a, 0)), dst_ref=part(i, slot(a, b)),
            send_sem=col_send.at[direction, which, i], recv_sem=col_recv.at[direction, which, i],
            device_id=(r, c - b), device_id_type=MESH)

    def row_starts(i):
        for ch in (0, 1):
            when(channels[ch][2], lambda: row_copy(ch, i).start())

    def col_sends(which, i):
        pl.when(jnp.logical_and(has_right, odd))(lambda: col_copy(0, which, i).start())
        when(has_left, lambda: col_copy(1, which, i).start())
        pl.when(jnp.logical_and(has_right, jnp.logical_not(odd)))(lambda: col_copy(0, which, i).start())

    depth = ROW_DEPTH if ring else chunks

    @pl.loop(0, chunks)
    def _(i):
        @pl.when(i < depth)
        def _():
            if ring:
                row_copy(0, i).start()
            else:
                row_starts(i)

        pl.when(i < COL_DEPTH)(lambda: col_sends(0, i))

    def first(i):
        def step():
            row_copy(0, i).wait_recv()
            if ring:
                when(channels[1][2], lambda: row_copy(1, i).start())
                pl.when(i + depth < chunks)(lambda: row_copy(0, i + depth).start())
            col_sends(1, i)
        when(channels[0][0], step)
        pl.when(i + COL_DEPTH < chunks)(lambda: col_sends(0, i + COL_DEPTH))

    def second(i):
        def step():
            row_copy(1, i).wait_recv()
            col_sends(2, i)
        when(channels[1][0], step)

    def forward(i):
        first(i)
        pl.when(i > 0)(lambda: second(i - 1))

    own = tissue[r, c].astype(jnp.float32)
    own = tissue[r, c].astype(jnp.float32)

    def compute(i):
        for direction, cond in ((0, has_left), (1, has_right)):
            for which in (0, 1, 2):
                there = cond
                if which and channels[which - 1][0] is not None:
                    there = jnp.logical_and(cond, channels[which - 1][0])
                when(there, lambda: col_copy(direction, which, i).wait_recv())
        queries = qt[i]
        scores = []
        for s, shift in enumerate(shifts):
            tile = jnp.dot(kv[i, 0, s], queries, preferred_element_type=jnp.float32)
            scores.append(tile if shift is None else tile + shift)
        top = jnp.max(functools.reduce(jnp.maximum, scores), axis=0, keepdims=True)
        weights = [jnp.exp(tile - top) for tile in scores]
        totals = jnp.sum(functools.reduce(jnp.add, weights), axis=0, keepdims=True)
        rounded = jnp.concatenate([tile.astype(jnp.bfloat16) for tile in weights], axis=0)
        values = jnp.concatenate([kv[i, 1, s] for s in range(9)], axis=1)
        mixed = jnp.dot(values, rounded, preferred_element_type=jnp.float32)
        mixed = mixed / totals * own
        mixed = jnp.concatenate([mixed[:HDIM, :tokens], mixed[HDIM:, tokens:]], axis=0)
        out_ref[0, 0, :, lanes(i)] = mixed.T.astype(out_ref.dtype)

    @pl.loop(0, LAG)
    def _(i):
        forward(i)

    @pl.loop(LAG, chunks)
    def _(i):
        forward(i)
        compute(i - LAG)

    second(chunks - 1)

    @pl.loop(chunks - LAG, chunks)
    def _(i):
        compute(i)

    @pl.loop(0, chunks)
    def _(i):
        for ch in (0, 1):
            when(channels[ch][2], lambda: row_copy(ch, i).wait_send())
        for which in (0, 1, 2):
            for direction, cond in ((0, has_right), (1, has_left)):
                there = cond
                if which and channels[which - 1][0] is not None:
                    there = jnp.logical_and(cond, channels[which - 1][0])
                when(there, lambda: col_copy(direction, which, i).wait_send())


def on_device(rows, cols, query_states, key_states, value_states, tissue_map):
    _, _, tokens, features = query_states.shape
    chunks = features // LANES
    in_hbm = pl.BlockSpec(memory_space=pltpu.HBM)
    return pl.pallas_call(
        functools.partial(kernel, rows, cols),
        out_shape=pltpu.VMEM(query_states.shape, jnp.bfloat16),
        in_specs=[in_hbm] * 4,
        out_specs=pl.BlockSpec(memory_space=pltpu.VMEM),
        scratch_shapes=[
            pltpu.VMEM((chunks, 2, 9, tokens, LANES), jnp.bfloat16),
            pltpu.VMEM((2, chunks, tokens, LANES), jnp.bfloat16),
            pltpu.VMEM((chunks, LANES, 2 * tokens), jnp.bfloat16),
            pltpu.SMEM(tissue_map.shape, jnp.int32),
            pltpu.SemaphoreType.DMA((3, chunks)),
            pltpu.SemaphoreType.DMA,
            pltpu.SemaphoreType.DMA((2, chunks)),
            pltpu.SemaphoreType.DMA((2, chunks)),
            pltpu.SemaphoreType.DMA((2, 3, chunks)),
            pltpu.SemaphoreType.DMA((2, 3, chunks)),
        ],
        compiler_params=pltpu.CompilerParams(
            collective_id=0, has_side_effects=True, vmem_limit_bytes=60 * 1024 * 1024),
        cost_estimate=pl.CostEstimate(
            flops=4 * 9 * tokens * tokens * features, bytes_accessed=8 * tokens * features,
            transcendentals=9 * tokens * tokens * features // HDIM),
        name="neighbourhood",
    )(tissue_map, query_states, key_states, value_states)


def solution(mesh):
    return jax.shard_map(
        functools.partial(on_device, mesh.shape["row"], mesh.shape["col"]),
        mesh=mesh,
        in_specs=(
            P("row", "col", None, None),
            P("row", "col", None, None),
            P("row", "col", None, None),
            P(),
        ),
        out_specs=P("row", "col", None, None),
        check_vma=False,
    )
```

```python
import functools

import jax
import jax.numpy as jnp
from jax import lax
from jax.experimental import pallas as pl
from jax.experimental.pallas import tpu as pltpu
from jax.sharding import PartitionSpec as P

HDIM = 64
LANES = 128
MESH = pl.DeviceIdType.MESH
LAG = 3
ROW_DEPTH = 3
COL_DEPTH = 2


def kernel(rows, cols, tissue_hbm, q_hbm, k_hbm, v_hbm, out_ref, kv, raw, qt, tissue, local_sem,
           tissue_sem, row_send, row_recv, col_send, col_recv):
    chunks, _, _, tokens, _ = kv.shape
    r, c = lax.axis_index("row"), lax.axis_index("col")
    ring = rows == 4
    has_up, has_down = r > 0, r < rows - 1
    has_left, has_right = c > 0, c < cols - 1
    slot = lambda a, b: (a + 1) * 3 + b + 1
    part = lambda i, s: kv.at[i, :, s]

    def lanes(i):
        return pl.ds(pl.multiple_of(i * LANES, LANES), LANES)

    def local_copies(i):
        return [
            pltpu.make_async_copy(k_hbm.at[0, 0, :, lanes(i)], kv.at[i, 0, 4], local_sem.at[0, i]),
            pltpu.make_async_copy(v_hbm.at[0, 0, :, lanes(i)], raw.at[1, i], local_sem.at[1, i]),
            pltpu.make_async_copy(q_hbm.at[0, 0, :, lanes(i)], raw.at[0, i], local_sem.at[2, i]),
        ]

    tissue_copy = pltpu.make_async_copy(tissue_hbm, tissue, tissue_sem)
    tissue_copy.start()

    if ring:
        near = 1 - 2 * lax.rem(r, 2)
        outer = jnp.logical_or(r == 0, r == 3)
        inner = jnp.logical_and(r > 0, r < 3)
        across = jnp.where(r < 2, r + 2, r - 2)
        channels = [
            (None, near, None, r + near, slot(0, 0), slot(-near, 0)),
            (inner, -near, outer, across, slot(near, 0), slot(-near, 0)),
        ]
        greet = [(None, r + near), (None, across)]
    else:
        channels = [
            (has_up, -1, has_down, r + 1, slot(0, 0), slot(-1, 0)),
            (has_down, 1, has_up, r - 1, slot(0, 0), slot(1, 0)),
        ]
        greet = [(has_up, r - 1), (has_down, r + 1)]

    def when(cond, f):
        if cond is None:
            f()
        else:
            pl.when(cond)(f)

    barrier = pltpu.get_barrier_semaphore()
    count = 0
    for cond, other in greet:
        when(cond, lambda other=other: pl.semaphore_signal(
            barrier, inc=1, device_id=(other, c), device_id_type=MESH))
        count = count + (1 if cond is None else cond.astype(jnp.int32))
    for cond, other in ((has_left, c - 1), (has_right, c + 1)):
        when(cond, lambda other=other: pl.semaphore_signal(
            barrier, inc=1, device_id=(r, other), device_id_type=MESH))
        count = count + cond.astype(jnp.int32)

    @pl.loop(0, chunks)
    def _(i):
        for copy in local_copies(i):
            copy.start()

    tissue_copy.wait()
    shifts = []
    for a in (-1, 0, 1):
        for b in (-1, 0, 1):
            s = slot(a, b)
            if (a, b) == (0, 0):
                shifts.append(None)
                continue
            inside = jnp.logical_and(jnp.logical_and(r + a >= 0, r + a < rows),
                                     jnp.logical_and(c + b >= 0, c + b < cols))
            entry = tissue[jnp.clip(r + a, 0, rows - 1), jnp.clip(c + b, 0, cols - 1)]
            live = jnp.where(inside, entry, 0) > 0
            shifts.append(jnp.where(live, jnp.float32(0), jnp.float32(-jnp.inf)))

            @pl.when(jnp.logical_not(inside))
            def _():
                @pl.loop(0, chunks)
                def _(i):
                    kv[i, :, s] = jnp.zeros((2, tokens, LANES), kv.dtype)

    pl.semaphore_wait(barrier, count)

    def row_copy(ch, i):
        _, _, _, target, source, landing = channels[ch]
        return pltpu.make_async_remote_copy(
            src_ref=part(i, source), dst_ref=part(i, landing),
            send_sem=row_send.at[ch, i], recv_sem=row_recv.at[ch, i],
            device_id=(target, c), device_id_type=MESH)

    def col_copy(direction, which, i):
        a = 0 if which == 0 else channels[which - 1][1]
        b = -1 if direction == 0 else 1
        return pltpu.make_async_remote_copy(
            src_ref=part(i, slot(a, 0)), dst_ref=part(i, slot(a, b)),
            send_sem=col_send.at[direction, which, i], recv_sem=col_recv.at[direction, which, i],
            device_id=(r, c - b), device_id_type=MESH)

    def row_starts(i):
        for ch in (0, 1):
            when(channels[ch][2], lambda: row_copy(ch, i).start())

    def col_sends(which, i):
        when(has_right, lambda: col_copy(0, which, i).start())
        when(has_left, lambda: col_copy(1, which, i).start())

    depth = ROW_DEPTH if ring else chunks

    @pl.loop(0, chunks)
    def _(i):
        for copy in local_copies(i)[:2]:
            copy.wait()
        kv[i, 1, 4] = raw[1, i].T

        @pl.when(i < depth)
        def _():
            if ring:
                row_copy(0, i).start()
            else:
                row_starts(i)

        pl.when(i < COL_DEPTH)(lambda: col_sends(0, i))

    low = lax.broadcasted_iota(jnp.int32, (LANES, tokens), 0) < HDIM

    @pl.loop(0, chunks)
    def _(i):
        local_copies(i)[2].wait()
        q = (raw[0, i] * jnp.bfloat16(HDIM ** -0.5)).T
        zero = jnp.zeros_like(q)
        qt[i, :, :tokens] = jnp.where(low, q, zero)
        qt[i, :, tokens:] = jnp.where(low, zero, q)

    def first(i):
        def step():
            row_copy(0, i).wait_recv()
            if ring:
                when(channels[1][2], lambda: row_copy(1, i).start())
                pl.when(i + depth < chunks)(lambda: row_copy(0, i + depth).start())
            col_sends(1, i)
        when(channels[0][0], step)
        pl.when(i + COL_DEPTH < chunks)(lambda: col_sends(0, i + COL_DEPTH))

    def second(i):
        def step():
            row_copy(1, i).wait_recv()
            col_sends(2, i)
        when(channels[1][0], step)

    def forward(i):
        first(i)
        pl.when(i > 0)(lambda: second(i - 1))

    own = tissue[r, c].astype(jnp.float32)
    own = tissue[r, c].astype(jnp.float32)

    def compute(i):
        for direction, cond in ((0, has_left), (1, has_right)):
            for which in (0, 1, 2):
                there = cond
                if which and channels[which - 1][0] is not None:
                    there = jnp.logical_and(cond, channels[which - 1][0])
                when(there, lambda: col_copy(direction, which, i).wait_recv())
        queries = qt[i]
        scores = []
        for s, shift in enumerate(shifts):
            tile = jnp.dot(kv[i, 0, s], queries, preferred_element_type=jnp.float32)
            scores.append(tile if shift is None else tile + shift)
        top = jnp.max(functools.reduce(jnp.maximum, scores), axis=0, keepdims=True)
        weights = [jnp.exp(tile - top) for tile in scores]
        totals = jnp.sum(functools.reduce(jnp.add, weights), axis=0, keepdims=True)
        rounded = jnp.concatenate([tile.astype(jnp.bfloat16) for tile in weights], axis=0)
        values = jnp.concatenate([kv[i, 1, s] for s in range(9)], axis=1)
        mixed = jnp.dot(values, rounded, preferred_element_type=jnp.float32)
        mixed = mixed / totals * own
        mixed = jnp.concatenate([mixed[:HDIM, :tokens], mixed[HDIM:, tokens:]], axis=0)
        out_ref[0, 0, :, lanes(i)] = mixed.T.astype(out_ref.dtype)

    @pl.loop(0, LAG)
    def _(i):
        forward(i)

    @pl.loop(LAG, chunks)
    def _(i):
        forward(i)
        when(inner if ring else None, lambda: compute(i - LAG))

    second(chunks - 1)

    begin = jnp.where(inner, chunks - LAG, 0) if ring else chunks - LAG

    @pl.loop(begin, chunks)
    def _(i):
        compute(i)

    @pl.loop(0, chunks)
    def _(i):
        for ch in (0, 1):
            when(channels[ch][2], lambda: row_copy(ch, i).wait_send())
        for which in (0, 1, 2):
            for direction, cond in ((0, has_right), (1, has_left)):
                there = cond
                if which and channels[which - 1][0] is not None:
                    there = jnp.logical_and(cond, channels[which - 1][0])
                when(there, lambda: col_copy(direction, which, i).wait_send())


def on_device(rows, cols, query_states, key_states, value_states, tissue_map):
    _, _, tokens, features = query_states.shape
    chunks = features // LANES
    in_hbm = pl.BlockSpec(memory_space=pltpu.HBM)
    return pl.pallas_call(
        functools.partial(kernel, rows, cols),
        out_shape=pltpu.VMEM(query_states.shape, jnp.bfloat16),
        in_specs=[in_hbm] * 4,
        out_specs=pl.BlockSpec(memory_space=pltpu.VMEM),
        scratch_shapes=[
            pltpu.VMEM((chunks, 2, 9, tokens, LANES), jnp.bfloat16),
            pltpu.VMEM((2, chunks, tokens, LANES), jnp.bfloat16),
            pltpu.VMEM((chunks, LANES, 2 * tokens), jnp.bfloat16),
            pltpu.SMEM(tissue_map.shape, jnp.int32),
            pltpu.SemaphoreType.DMA((3, chunks)),
            pltpu.SemaphoreType.DMA,
            pltpu.SemaphoreType.DMA((2, chunks)),
            pltpu.SemaphoreType.DMA((2, chunks)),
            pltpu.SemaphoreType.DMA((2, 3, chunks)),
            pltpu.SemaphoreType.DMA((2, 3, chunks)),
        ],
        compiler_params=pltpu.CompilerParams(
            collective_id=0, has_side_effects=True, vmem_limit_bytes=60 * 1024 * 1024),
        cost_estimate=pl.CostEstimate(
            flops=4 * 9 * tokens * tokens * features, bytes_accessed=8 * tokens * features,
            transcendentals=9 * tokens * tokens * features // HDIM),
        name="neighbourhood",
    )(tissue_map, query_states, key_states, value_states)


def solution(mesh):
    return jax.shard_map(
        functools.partial(on_device, mesh.shape["row"], mesh.shape["col"]),
        mesh=mesh,
        in_specs=(
            P("row", "col", None, None),
            P("row", "col", None, None),
            P("row", "col", None, None),
            P(),
        ),
        out_specs=P("row", "col", None, None),
        check_vma=False,
    )
```

```python
import functools

import jax
import jax.numpy as jnp
from jax import lax
from jax.experimental import pallas as pl
from jax.experimental.pallas import tpu as pltpu
from jax.sharding import PartitionSpec as P

HDIM = 64
LANES = 128
MESH = pl.DeviceIdType.MESH
LAG = 4
ROW_DEPTH = 3
COL_DEPTH = 6


def kernel(rows, cols, tissue_hbm, q_hbm, k_hbm, v_hbm, out_ref, kv, raw, qt, tissue, local_sem,
           tissue_sem, row_send, row_recv, col_send, col_recv):
    chunks, _, _, tokens, _ = kv.shape
    r, c = lax.axis_index("row"), lax.axis_index("col")
    ring = rows == 4
    has_up, has_down = r > 0, r < rows - 1
    has_left, has_right = c > 0, c < cols - 1
    slot = lambda a, b: (a + 1) * 3 + b + 1
    part = lambda i, s: kv.at[i, :, s]

    def lanes(i):
        return pl.ds(pl.multiple_of(i * LANES, LANES), LANES)

    def local_copies(i):
        return [
            pltpu.make_async_copy(k_hbm.at[0, 0, :, lanes(i)], kv.at[i, 0, 4], local_sem.at[0, i]),
            pltpu.make_async_copy(v_hbm.at[0, 0, :, lanes(i)], raw.at[1, i], local_sem.at[1, i]),
            pltpu.make_async_copy(q_hbm.at[0, 0, :, lanes(i)], raw.at[0, i], local_sem.at[2, i]),
        ]

    tissue_copy = pltpu.make_async_copy(tissue_hbm, tissue, tissue_sem)
    tissue_copy.start()

    if ring:
        near = 1 - 2 * lax.rem(r, 2)
        outer = jnp.logical_or(r == 0, r == 3)
        inner = jnp.logical_and(r > 0, r < 3)
        across = jnp.where(r < 2, r + 2, r - 2)
        channels = [
            (None, near, None, r + near, slot(0, 0), slot(-near, 0)),
            (inner, -near, outer, across, slot(near, 0), slot(-near, 0)),
        ]
        greet = [(None, r + near), (None, across)]
    else:
        channels = [
            (has_up, -1, has_down, r + 1, slot(0, 0), slot(-1, 0)),
            (has_down, 1, has_up, r - 1, slot(0, 0), slot(1, 0)),
        ]
        greet = [(has_up, r - 1), (has_down, r + 1)]

    def when(cond, f):
        if cond is None:
            f()
        else:
            pl.when(cond)(f)

    barrier = pltpu.get_barrier_semaphore()
    count = 0
    for cond, other in greet:
        when(cond, lambda other=other: pl.semaphore_signal(
            barrier, inc=1, device_id=(other, c), device_id_type=MESH))
        count = count + (1 if cond is None else cond.astype(jnp.int32))
    for cond, other in ((has_left, c - 1), (has_right, c + 1)):
        when(cond, lambda other=other: pl.semaphore_signal(
            barrier, inc=1, device_id=(r, other), device_id_type=MESH))
        count = count + cond.astype(jnp.int32)

    @pl.loop(0, chunks)
    def _(i):
        for copy in local_copies(i):
            copy.start()

    tissue_copy.wait()
    shifts = []
    for a in (-1, 0, 1):
        for b in (-1, 0, 1):
            s = slot(a, b)
            if (a, b) == (0, 0):
                shifts.append(None)
                continue
            inside = jnp.logical_and(jnp.logical_and(r + a >= 0, r + a < rows),
                                     jnp.logical_and(c + b >= 0, c + b < cols))
            entry = tissue[jnp.clip(r + a, 0, rows - 1), jnp.clip(c + b, 0, cols - 1)]
            live = jnp.where(inside, entry, 0) > 0
            shifts.append(jnp.where(live, jnp.float32(0), jnp.float32(-jnp.inf)))

            @pl.when(jnp.logical_not(inside))
            def _():
                @pl.loop(0, chunks)
                def _(i):
                    kv[i, :, s] = jnp.zeros((2, tokens, LANES), kv.dtype)

    pl.semaphore_wait(barrier, count)

    def row_copy(ch, i):
        _, _, _, target, source, landing = channels[ch]
        return pltpu.make_async_remote_copy(
            src_ref=part(i, source), dst_ref=part(i, landing),
            send_sem=row_send.at[ch, i], recv_sem=row_recv.at[ch, i],
            device_id=(target, c), device_id_type=MESH)

    def col_copy(direction, which, i):
        a = 0 if which == 0 else channels[which - 1][1]
        b = -1 if direction == 0 else 1
        return pltpu.make_async_remote_copy(
            src_ref=part(i, slot(a, 0)), dst_ref=part(i, slot(a, b)),
            send_sem=col_send.at[direction, which, i], recv_sem=col_recv.at[direction, which, i],
            device_id=(r, c - b), device_id_type=MESH)

    def row_starts(i):
        for ch in (0, 1):
            when(channels[ch][2], lambda: row_copy(ch, i).start())

    def col_sends(which, i):
        when(has_right, lambda: col_copy(0, which, i).start())
        when(has_left, lambda: col_copy(1, which, i).start())

    depth = ROW_DEPTH if ring else chunks

    @pl.loop(0, chunks)
    def _(i):
        for copy in local_copies(i)[:2]:
            copy.wait()
        kv[i, 1, 4] = raw[1, i].T

        @pl.when(i < depth)
        def _():
            if ring:
                row_copy(0, i).start()
            else:
                row_starts(i)

        pl.when(i < COL_DEPTH)(lambda: col_sends(0, i))

    low = lax.broadcasted_iota(jnp.int32, (LANES, tokens), 0) < HDIM

    @pl.loop(0, chunks)
    def _(i):
        local_copies(i)[2].wait()
        q = (raw[0, i] * jnp.bfloat16(HDIM ** -0.5)).T
        zero = jnp.zeros_like(q)
        qt[i, :, :tokens] = jnp.where(low, q, zero)
        qt[i, :, tokens:] = jnp.where(low, zero, q)

    def first(i):
        def step():
            row_copy(0, i).wait_recv()
            if ring:
                when(channels[1][2], lambda: row_copy(1, i).start())
                pl.when(i + depth < chunks)(lambda: row_copy(0, i + depth).start())
            col_sends(1, i)
        when(channels[0][0], step)
        pl.when(i + COL_DEPTH < chunks)(lambda: col_sends(0, i + COL_DEPTH))

    def second(i):
        def step():
            row_copy(1, i).wait_recv()
            col_sends(2, i)
        when(channels[1][0], step)

    def forward(i):
        first(i)
        pl.when(i > 0)(lambda: second(i - 1))

    own = tissue[r, c].astype(jnp.float32)
    own = tissue[r, c].astype(jnp.float32)

    def compute(i):
        for direction, cond in ((0, has_left), (1, has_right)):
            for which in (0, 1, 2):
                there = cond
                if which and channels[which - 1][0] is not None:
                    there = jnp.logical_and(cond, channels[which - 1][0])
                when(there, lambda: col_copy(direction, which, i).wait_recv())
        queries = qt[i]
        scores = []
        for s, shift in enumerate(shifts):
            tile = jnp.dot(kv[i, 0, s], queries, preferred_element_type=jnp.float32)
            scores.append(tile if shift is None else tile + shift)
        top = jnp.max(functools.reduce(jnp.maximum, scores), axis=0, keepdims=True)
        weights = [jnp.exp(tile - top) for tile in scores]
        totals = jnp.sum(functools.reduce(jnp.add, weights), axis=0, keepdims=True)
        rounded = jnp.concatenate([tile.astype(jnp.bfloat16) for tile in weights], axis=0)
        values = jnp.concatenate([kv[i, 1, s] for s in range(9)], axis=1)
        mixed = jnp.dot(values, rounded, preferred_element_type=jnp.float32)
        mixed = mixed / totals * own
        mixed = jnp.concatenate([mixed[:HDIM, :tokens], mixed[HDIM:, tokens:]], axis=0)
        out_ref[0, 0, :, lanes(i)] = mixed.T.astype(out_ref.dtype)

    @pl.loop(0, LAG)
    def _(i):
        forward(i)

    @pl.loop(LAG, chunks)
    def _(i):
        forward(i)
        when(inner if ring else None, lambda: compute(i - LAG))

    second(chunks - 1)

    begin = jnp.where(inner, chunks - LAG, 0) if ring else chunks - LAG

    @pl.loop(begin, chunks)
    def _(i):
        compute(i)

    @pl.loop(0, chunks)
    def _(i):
        for ch in (0, 1):
            when(channels[ch][2], lambda: row_copy(ch, i).wait_send())
        for which in (0, 1, 2):
            for direction, cond in ((0, has_right), (1, has_left)):
                there = cond
                if which and channels[which - 1][0] is not None:
                    there = jnp.logical_and(cond, channels[which - 1][0])
                when(there, lambda: col_copy(direction, which, i).wait_send())


def on_device(rows, cols, query_states, key_states, value_states, tissue_map):
    _, _, tokens, features = query_states.shape
    chunks = features // LANES
    in_hbm = pl.BlockSpec(memory_space=pltpu.HBM)
    return pl.pallas_call(
        functools.partial(kernel, rows, cols),
        out_shape=pltpu.VMEM(query_states.shape, jnp.bfloat16),
        in_specs=[in_hbm] * 4,
        out_specs=pl.BlockSpec(memory_space=pltpu.VMEM),
        scratch_shapes=[
            pltpu.VMEM((chunks, 2, 9, tokens, LANES), jnp.bfloat16),
            pltpu.VMEM((2, chunks, tokens, LANES), jnp.bfloat16),
            pltpu.VMEM((chunks, LANES, 2 * tokens), jnp.bfloat16),
            pltpu.SMEM(tissue_map.shape, jnp.int32),
            pltpu.SemaphoreType.DMA((3, chunks)),
            pltpu.SemaphoreType.DMA,
            pltpu.SemaphoreType.DMA((2, chunks)),
            pltpu.SemaphoreType.DMA((2, chunks)),
            pltpu.SemaphoreType.DMA((2, 3, chunks)),
            pltpu.SemaphoreType.DMA((2, 3, chunks)),
        ],
        compiler_params=pltpu.CompilerParams(
            collective_id=0, has_side_effects=True, vmem_limit_bytes=60 * 1024 * 1024),
        cost_estimate=pl.CostEstimate(
            flops=4 * 9 * tokens * tokens * features, bytes_accessed=8 * tokens * features,
            transcendentals=9 * tokens * tokens * features // HDIM),
        name="neighbourhood",
    )(tissue_map, query_states, key_states, value_states)


def solution(mesh):
    return jax.shard_map(
        functools.partial(on_device, mesh.shape["row"], mesh.shape["col"]),
        mesh=mesh,
        in_specs=(
            P("row", "col", None, None),
            P("row", "col", None, None),
            P("row", "col", None, None),
            P(),
        ),
        out_specs=P("row", "col", None, None),
        check_vma=False,
    )
```

```python
import functools

import jax
import jax.numpy as jnp
from jax import lax
from jax.experimental import pallas as pl
from jax.experimental.pallas import tpu as pltpu
from jax.sharding import PartitionSpec as P

HDIM = 64
LANES = 128
MESH = pl.DeviceIdType.MESH
LAG = 4
ROW_DEPTH = 3
COL_DEPTH = 6


def kernel(rows, cols, tissue_hbm, q_hbm, k_hbm, v_hbm, out_ref, kv, raw, qt, tissue, local_sem,
           tissue_sem, row_send, row_recv, col_send, col_recv):
    chunks, _, _, tokens, _ = kv.shape
    r, c = lax.axis_index("row"), lax.axis_index("col")
    ring = rows == 4
    has_up, has_down = r > 0, r < rows - 1
    has_left, has_right = c > 0, c < cols - 1
    slot = lambda a, b: (a + 1) * 3 + b + 1
    part = lambda i, s: kv.at[i, :, s]

    def lanes(i):
        return pl.ds(pl.multiple_of(i * LANES, LANES), LANES)

    def local_copies(i):
        return [
            pltpu.make_async_copy(k_hbm.at[0, 0, :, lanes(i)], kv.at[i, 0, 4], local_sem.at[0, i]),
            pltpu.make_async_copy(v_hbm.at[0, 0, :, lanes(i)], raw.at[1, i], local_sem.at[1, i]),
            pltpu.make_async_copy(q_hbm.at[0, 0, :, lanes(i)], raw.at[0, i], local_sem.at[2, i]),
        ]

    tissue_copy = pltpu.make_async_copy(tissue_hbm, tissue, tissue_sem)
    tissue_copy.start()

    if ring:
        near = 1 - 2 * lax.rem(r, 2)
        outer = jnp.logical_or(r == 0, r == 3)
        inner = jnp.logical_and(r > 0, r < 3)
        across = jnp.where(r < 2, r + 2, r - 2)
        channels = [
            (None, near, None, r + near, slot(0, 0), slot(-near, 0)),
            (inner, -near, outer, across, slot(near, 0), slot(-near, 0)),
        ]
        greet = [(None, r + near), (None, across)]
    else:
        channels = [
            (has_up, -1, has_down, r + 1, slot(0, 0), slot(-1, 0)),
            (has_down, 1, has_up, r - 1, slot(0, 0), slot(1, 0)),
        ]
        greet = [(has_up, r - 1), (has_down, r + 1)]

    def when(cond, f):
        if cond is None:
            f()
        else:
            pl.when(cond)(f)

    barrier = pltpu.get_barrier_semaphore()
    count = 0
    for cond, other in greet:
        when(cond, lambda other=other: pl.semaphore_signal(
            barrier, inc=1, device_id=(other, c), device_id_type=MESH))
        count = count + (1 if cond is None else cond.astype(jnp.int32))
    for cond, other in ((has_left, c - 1), (has_right, c + 1)):
        when(cond, lambda other=other: pl.semaphore_signal(
            barrier, inc=1, device_id=(r, other), device_id_type=MESH))
        count = count + cond.astype(jnp.int32)

    @pl.loop(0, chunks)
    def _(i):
        for copy in local_copies(i):
            copy.start()

    tissue_copy.wait()
    shifts = []
    for a in (-1, 0, 1):
        for b in (-1, 0, 1):
            s = slot(a, b)
            if (a, b) == (0, 0):
                shifts.append(None)
                continue
            inside = jnp.logical_and(jnp.logical_and(r + a >= 0, r + a < rows),
                                     jnp.logical_and(c + b >= 0, c + b < cols))
            entry = tissue[jnp.clip(r + a, 0, rows - 1), jnp.clip(c + b, 0, cols - 1)]
            live = jnp.where(inside, entry, 0) > 0
            shifts.append(jnp.where(live, jnp.float32(0), jnp.float32(-jnp.inf)))

            @pl.when(jnp.logical_not(inside))
            def _():
                @pl.loop(0, chunks)
                def _(i):
                    kv[i, :, s] = jnp.zeros((2, tokens, LANES), kv.dtype)

    pl.semaphore_wait(barrier, count)

    def row_copy(ch, i):
        _, _, _, target, source, landing = channels[ch]
        return pltpu.make_async_remote_copy(
            src_ref=part(i, source), dst_ref=part(i, landing),
            send_sem=row_send.at[ch, i], recv_sem=row_recv.at[ch, i],
            device_id=(target, c), device_id_type=MESH)

    def col_copy(direction, which, i):
        a = 0 if which == 0 else channels[which - 1][1]
        b = -1 if direction == 0 else 1
        return pltpu.make_async_remote_copy(
            src_ref=part(i, slot(a, 0)), dst_ref=part(i, slot(a, b)),
            send_sem=col_send.at[direction, which, i], recv_sem=col_recv.at[direction, which, i],
            device_id=(r, c - b), device_id_type=MESH)

    def row_starts(i):
        for ch in (0, 1):
            when(channels[ch][2], lambda: row_copy(ch, i).start())

    def col_sends(which, i):
        when(has_right, lambda: col_copy(0, which, i).start())
        when(has_left, lambda: col_copy(1, which, i).start())

    depth = ROW_DEPTH if ring else chunks

    @pl.loop(0, chunks)
    def _(i):
        for copy in local_copies(i)[:2]:
            copy.wait()
        kv[i, 1, 4] = raw[1, i].T

        @pl.when(i < depth)
        def _():
            if ring:
                row_copy(0, i).start()
            else:
                row_starts(i)

        pl.when(i < COL_DEPTH)(lambda: col_sends(0, i))

    low = lax.broadcasted_iota(jnp.int32, (LANES, tokens), 0) < HDIM

    @pl.loop(0, chunks)
    def _(i):
        local_copies(i)[2].wait()
        q = (raw[0, i] * jnp.bfloat16(HDIM ** -0.5)).T
        zero = jnp.zeros_like(q)
        qt[i, :, :tokens] = jnp.where(low, q, zero)
        qt[i, :, tokens:] = jnp.where(low, zero, q)

    def first(i):
        def step():
            row_copy(0, i).wait_recv()
            if ring:
                when(channels[1][2], lambda: row_copy(1, i).start())
                pl.when(i + depth < chunks)(lambda: row_copy(0, i + depth).start())
            col_sends(1, i)
        when(channels[0][0], step)
        pl.when(i + COL_DEPTH < chunks)(lambda: col_sends(0, i + COL_DEPTH))

    def second(i):
        def step():
            row_copy(1, i).wait_recv()
            col_sends(2, i)
        when(channels[1][0], step)

    def forward(i):
        first(i)
        pl.when(i > 0)(lambda: second(i - 1))

    own = tissue[r, c].astype(jnp.float32)
    own = tissue[r, c].astype(jnp.float32)

    def compute(i):
        for direction, cond in ((0, has_left), (1, has_right)):
            for which in (0, 1, 2):
                there = cond
                if which and channels[which - 1][0] is not None:
                    there = jnp.logical_and(cond, channels[which - 1][0])
                when(there, lambda: col_copy(direction, which, i).wait_recv())
        queries = qt[i]
        scores = []
        for s, shift in enumerate(shifts):
            tile = jnp.dot(kv[i, 0, s], queries, preferred_element_type=jnp.float32)
            scores.append(tile if shift is None else tile + shift)
        top = jnp.max(functools.reduce(jnp.maximum, scores), axis=0, keepdims=True)
        weights = [jnp.exp(tile - top) for tile in scores]
        totals = jnp.sum(functools.reduce(jnp.add, weights), axis=0, keepdims=True)
        rounded = jnp.concatenate([tile.astype(jnp.bfloat16) for tile in weights], axis=0)
        values = jnp.concatenate([kv[i, 1, s] for s in range(9)], axis=1)
        mixed = jnp.dot(values, rounded, preferred_element_type=jnp.float32)
        mixed = mixed / totals * own
        mixed = jnp.concatenate([mixed[:HDIM, :tokens], mixed[HDIM:, tokens:]], axis=0)
        out_ref[0, 0, :, lanes(i)] = mixed.T.astype(out_ref.dtype)

    @pl.loop(0, LAG)
    def _(i):
        forward(i)

    @pl.loop(LAG, chunks)
    def _(i):
        forward(i)
        when(inner if ring else None, lambda: compute(i - LAG))

    when(inner if ring else None, lambda: compute(chunks - LAG))
    second(chunks - 1)

    begin = chunks - LAG + 1
    begin = jnp.where(inner, begin, 0) if ring else begin

    @pl.loop(begin, chunks)
    def _(i):
        compute(i)

    @pl.loop(0, chunks)
    def _(i):
        for ch in (0, 1):
            when(channels[ch][2], lambda: row_copy(ch, i).wait_send())
        for which in (0, 1, 2):
            for direction, cond in ((0, has_right), (1, has_left)):
                there = cond
                if which and channels[which - 1][0] is not None:
                    there = jnp.logical_and(cond, channels[which - 1][0])
                when(there, lambda: col_copy(direction, which, i).wait_send())


def on_device(rows, cols, query_states, key_states, value_states, tissue_map):
    _, _, tokens, features = query_states.shape
    chunks = features // LANES
    in_hbm = pl.BlockSpec(memory_space=pltpu.HBM)
    return pl.pallas_call(
        functools.partial(kernel, rows, cols),
        out_shape=pltpu.VMEM(query_states.shape, jnp.bfloat16),
        in_specs=[in_hbm] * 4,
        out_specs=pl.BlockSpec(memory_space=pltpu.VMEM),
        scratch_shapes=[
            pltpu.VMEM((chunks, 2, 9, tokens, LANES), jnp.bfloat16),
            pltpu.VMEM((2, chunks, tokens, LANES), jnp.bfloat16),
            pltpu.VMEM((chunks, LANES, 2 * tokens), jnp.bfloat16),
            pltpu.SMEM(tissue_map.shape, jnp.int32),
            pltpu.SemaphoreType.DMA((3, chunks)),
            pltpu.SemaphoreType.DMA,
            pltpu.SemaphoreType.DMA((2, chunks)),
            pltpu.SemaphoreType.DMA((2, chunks)),
            pltpu.SemaphoreType.DMA((2, 3, chunks)),
            pltpu.SemaphoreType.DMA((2, 3, chunks)),
        ],
        compiler_params=pltpu.CompilerParams(
            collective_id=0, has_side_effects=True, vmem_limit_bytes=60 * 1024 * 1024),
        cost_estimate=pl.CostEstimate(
            flops=4 * 9 * tokens * tokens * features, bytes_accessed=8 * tokens * features,
            transcendentals=9 * tokens * tokens * features // HDIM),
        name="neighbourhood",
    )(tissue_map, query_states, key_states, value_states)


def solution(mesh):
    return jax.shard_map(
        functools.partial(on_device, mesh.shape["row"], mesh.shape["col"]),
        mesh=mesh,
        in_specs=(
            P("row", "col", None, None),
            P("row", "col", None, None),
            P("row", "col", None, None),
            P(),
        ),
        out_specs=P("row", "col", None, None),
        check_vma=False,
    )
```

```python
import functools

import jax
import jax.numpy as jnp
from jax import lax
from jax.experimental import pallas as pl
from jax.experimental.pallas import tpu as pltpu
from jax.sharding import PartitionSpec as P

HDIM = 64
LANES = 128
MESH = pl.DeviceIdType.MESH
LAG = 5
ROW_DEPTH = 3
COL_DEPTH = 6


def kernel(rows, cols, tissue_hbm, q_hbm, k_hbm, v_hbm, out_ref, kv, raw, qt, tissue, local_sem,
           tissue_sem, row_send, row_recv, col_send, col_recv):
    chunks, _, _, tokens, _ = kv.shape
    r, c = lax.axis_index("row"), lax.axis_index("col")
    ring = rows == 4
    has_up, has_down = r > 0, r < rows - 1
    has_left, has_right = c > 0, c < cols - 1
    slot = lambda a, b: (a + 1) * 3 + b + 1
    part = lambda i, s: kv.at[i, :, s]

    def lanes(i):
        return pl.ds(pl.multiple_of(i * LANES, LANES), LANES)

    def local_copies(i):
        return [
            pltpu.make_async_copy(k_hbm.at[0, 0, :, lanes(i)], kv.at[i, 0, 4], local_sem.at[0, i]),
            pltpu.make_async_copy(v_hbm.at[0, 0, :, lanes(i)], raw.at[1, i], local_sem.at[1, i]),
            pltpu.make_async_copy(q_hbm.at[0, 0, :, lanes(i)], raw.at[0, i], local_sem.at[2, i]),
        ]

    tissue_copy = pltpu.make_async_copy(tissue_hbm, tissue, tissue_sem)
    tissue_copy.start()

    if ring:
        near = 1 - 2 * lax.rem(r, 2)
        outer = jnp.logical_or(r == 0, r == 3)
        inner = jnp.logical_and(r > 0, r < 3)
        across = jnp.where(r < 2, r + 2, r - 2)
        channels = [
            (None, near, None, r + near, slot(0, 0), slot(-near, 0)),
            (inner, -near, outer, across, slot(near, 0), slot(-near, 0)),
        ]
        greet = [(None, r + near), (None, across)]
    else:
        channels = [
            (has_up, -1, has_down, r + 1, slot(0, 0), slot(-1, 0)),
            (has_down, 1, has_up, r - 1, slot(0, 0), slot(1, 0)),
        ]
        greet = [(has_up, r - 1), (has_down, r + 1)]

    def when(cond, f):
        if cond is None:
            f()
        else:
            pl.when(cond)(f)

    barrier = pltpu.get_barrier_semaphore()
    count = 0
    for cond, other in greet:
        when(cond, lambda other=other: pl.semaphore_signal(
            barrier, inc=1, device_id=(other, c), device_id_type=MESH))
        count = count + (1 if cond is None else cond.astype(jnp.int32))
    for cond, other in ((has_left, c - 1), (has_right, c + 1)):
        when(cond, lambda other=other: pl.semaphore_signal(
            barrier, inc=1, device_id=(r, other), device_id_type=MESH))
        count = count + cond.astype(jnp.int32)

    @pl.loop(0, chunks)
    def _(i):
        for copy in local_copies(i):
            copy.start()

    tissue_copy.wait()
    shifts = []
    for a in (-1, 0, 1):
        for b in (-1, 0, 1):
            s = slot(a, b)
            if (a, b) == (0, 0):
                shifts.append(None)
                continue
            inside = jnp.logical_and(jnp.logical_and(r + a >= 0, r + a < rows),
                                     jnp.logical_and(c + b >= 0, c + b < cols))
            entry = tissue[jnp.clip(r + a, 0, rows - 1), jnp.clip(c + b, 0, cols - 1)]
            live = jnp.where(inside, entry, 0) > 0
            shifts.append(jnp.where(live, jnp.float32(0), jnp.float32(-jnp.inf)))

            @pl.when(jnp.logical_not(inside))
            def _():
                @pl.loop(0, chunks)
                def _(i):
                    kv[i, :, s] = jnp.zeros((2, tokens, LANES), kv.dtype)

    pl.semaphore_wait(barrier, count)

    def row_copy(ch, i):
        _, _, _, target, source, landing = channels[ch]
        return pltpu.make_async_remote_copy(
            src_ref=part(i, source), dst_ref=part(i, landing),
            send_sem=row_send.at[ch, i], recv_sem=row_recv.at[ch, i],
            device_id=(target, c), device_id_type=MESH)

    def col_copy(direction, which, i):
        a = 0 if which == 0 else channels[which - 1][1]
        b = -1 if direction == 0 else 1
        return pltpu.make_async_remote_copy(
            src_ref=part(i, slot(a, 0)), dst_ref=part(i, slot(a, b)),
            send_sem=col_send.at[direction, which, i], recv_sem=col_recv.at[direction, which, i],
            device_id=(r, c - b), device_id_type=MESH)

    def row_starts(i):
        for ch in (0, 1):
            when(channels[ch][2], lambda: row_copy(ch, i).start())

    def col_sends(which, i):
        when(has_right, lambda: col_copy(0, which, i).start())
        when(has_left, lambda: col_copy(1, which, i).start())

    depth = ROW_DEPTH if ring else chunks

    @pl.loop(0, chunks)
    def _(i):
        for copy in local_copies(i)[:2]:
            copy.wait()
        kv[i, 1, 4] = raw[1, i].T

        @pl.when(i < depth)
        def _():
            if ring:
                row_copy(0, i).start()
            else:
                row_starts(i)

        pl.when(i < COL_DEPTH)(lambda: col_sends(0, i))

    low = lax.broadcasted_iota(jnp.int32, (LANES, tokens), 0) < HDIM

    @pl.loop(0, chunks)
    def _(i):
        local_copies(i)[2].wait()
        q = (raw[0, i] * jnp.bfloat16(HDIM ** -0.5)).T
        zero = jnp.zeros_like(q)
        qt[i, :, :tokens] = jnp.where(low, q, zero)
        qt[i, :, tokens:] = jnp.where(low, zero, q)

    def first(i):
        def step():
            row_copy(0, i).wait_recv()
            if ring:
                when(channels[1][2], lambda: row_copy(1, i).start())
                pl.when(i + depth < chunks)(lambda: row_copy(0, i + depth).start())
            col_sends(1, i)
        when(channels[0][0], step)
        pl.when(i + COL_DEPTH < chunks)(lambda: col_sends(0, i + COL_DEPTH))

    def second(i):
        def step():
            row_copy(1, i).wait_recv()
            col_sends(2, i)
        when(channels[1][0], step)

    def forward(i):
        first(i)
        pl.when(i > 0)(lambda: second(i - 1))

    own = tissue[r, c].astype(jnp.float32)
    own = tissue[r, c].astype(jnp.float32)

    def compute(i):
        for direction, cond in ((0, has_left), (1, has_right)):
            for which in (0, 1, 2):
                there = cond
                if which and channels[which - 1][0] is not None:
                    there = jnp.logical_and(cond, channels[which - 1][0])
                when(there, lambda: col_copy(direction, which, i).wait_recv())
        queries = qt[i]
        scores = []
        for s, shift in enumerate(shifts):
            tile = jnp.dot(kv[i, 0, s], queries, preferred_element_type=jnp.float32)
            scores.append(tile if shift is None else tile + shift)
        top = jnp.max(functools.reduce(jnp.maximum, scores), axis=0, keepdims=True)
        weights = [jnp.exp(tile - top) for tile in scores]
        totals = jnp.sum(functools.reduce(jnp.add, weights), axis=0, keepdims=True)
        rounded = jnp.concatenate([tile.astype(jnp.bfloat16) for tile in weights], axis=0)
        values = jnp.concatenate([kv[i, 1, s] for s in range(9)], axis=1)
        mixed = jnp.dot(values, rounded, preferred_element_type=jnp.float32)
        mixed = mixed / totals * own
        mixed = jnp.concatenate([mixed[:HDIM, :tokens], mixed[HDIM:, tokens:]], axis=0)
        out_ref[0, 0, :, lanes(i)] = mixed.T.astype(out_ref.dtype)

    @pl.loop(0, LAG)
    def _(i):
        forward(i)

    @pl.loop(LAG, chunks)
    def _(i):
        forward(i)
        when(inner if ring else None, lambda: compute(i - LAG))

    second(chunks - 1)

    begin = jnp.where(inner, chunks - LAG, 0) if ring else chunks - LAG

    @pl.loop(begin, chunks)
    def _(i):
        compute(i)

    @pl.loop(0, chunks)
    def _(i):
        for ch in (0, 1):
            when(channels[ch][2], lambda: row_copy(ch, i).wait_send())
        for which in (0, 1, 2):
            for direction, cond in ((0, has_right), (1, has_left)):
                there = cond
                if which and channels[which - 1][0] is not None:
                    there = jnp.logical_and(cond, channels[which - 1][0])
                when(there, lambda: col_copy(direction, which, i).wait_send())


def on_device(rows, cols, query_states, key_states, value_states, tissue_map):
    _, _, tokens, features = query_states.shape
    chunks = features // LANES
    in_hbm = pl.BlockSpec(memory_space=pltpu.HBM)
    return pl.pallas_call(
        functools.partial(kernel, rows, cols),
        out_shape=pltpu.VMEM(query_states.shape, jnp.bfloat16),
        in_specs=[in_hbm] * 4,
        out_specs=pl.BlockSpec(memory_space=pltpu.VMEM),
        scratch_shapes=[
            pltpu.VMEM((chunks, 2, 9, tokens, LANES), jnp.bfloat16),
            pltpu.VMEM((2, chunks, tokens, LANES), jnp.bfloat16),
            pltpu.VMEM((chunks, LANES, 2 * tokens), jnp.bfloat16),
            pltpu.SMEM(tissue_map.shape, jnp.int32),
            pltpu.SemaphoreType.DMA((3, chunks)),
            pltpu.SemaphoreType.DMA,
            pltpu.SemaphoreType.DMA((2, chunks)),
            pltpu.SemaphoreType.DMA((2, chunks)),
            pltpu.SemaphoreType.DMA((2, 3, chunks)),
            pltpu.SemaphoreType.DMA((2, 3, chunks)),
        ],
        compiler_params=pltpu.CompilerParams(
            collective_id=0, has_side_effects=True, vmem_limit_bytes=60 * 1024 * 1024),
        cost_estimate=pl.CostEstimate(
            flops=4 * 9 * tokens * tokens * features, bytes_accessed=8 * tokens * features,
            transcendentals=9 * tokens * tokens * features // HDIM),
        name="neighbourhood",
    )(tissue_map, query_states, key_states, value_states)


def solution(mesh):
    return jax.shard_map(
        functools.partial(on_device, mesh.shape["row"], mesh.shape["col"]),
        mesh=mesh,
        in_specs=(
            P("row", "col", None, None),
            P("row", "col", None, None),
            P("row", "col", None, None),
            P(),
        ),
        out_specs=P("row", "col", None, None),
        check_vma=False,
    )
```

```python
import functools

import jax
import jax.numpy as jnp
from jax import lax
from jax.experimental import pallas as pl
from jax.experimental.pallas import tpu as pltpu
from jax.sharding import PartitionSpec as P

HDIM = 64
LANES = 128
MESH = pl.DeviceIdType.MESH
LAG = 4
ROW_DEPTH = 3
COL_DEPTH = 6


def kernel(rows, cols, tissue_hbm, q_hbm, k_hbm, v_hbm, out_ref, kv, raw, qt, tissue, local_sem,
           tissue_sem, row_send, row_recv, col_send, col_recv):
    chunks, _, _, tokens, _ = kv.shape
    r, c = lax.axis_index("row"), lax.axis_index("col")
    ring = rows == 4
    has_up, has_down = r > 0, r < rows - 1
    has_left, has_right = c > 0, c < cols - 1
    slot = lambda a, b: (a + 1) * 3 + b + 1
    part = lambda i, s: kv.at[i, :, s]

    def lanes(i):
        return pl.ds(pl.multiple_of(i * LANES, LANES), LANES)

    def local_copies(i):
        return [
            pltpu.make_async_copy(k_hbm.at[0, 0, :, lanes(i)], kv.at[i, 0, 4], local_sem.at[0, i]),
            pltpu.make_async_copy(v_hbm.at[0, 0, :, lanes(i)], raw.at[1, i], local_sem.at[1, i]),
            pltpu.make_async_copy(q_hbm.at[0, 0, :, lanes(i)], raw.at[0, i], local_sem.at[2, i]),
        ]

    tissue_copy = pltpu.make_async_copy(tissue_hbm, tissue, tissue_sem)
    tissue_copy.start()

    if ring:
        near = 1 - 2 * lax.rem(r, 2)
        outer = jnp.logical_or(r == 0, r == 3)
        inner = jnp.logical_and(r > 0, r < 3)
        across = jnp.where(r < 2, r + 2, r - 2)
        channels = [
            (None, near, None, r + near, slot(0, 0), slot(-near, 0)),
            (inner, -near, outer, across, slot(near, 0), slot(-near, 0)),
        ]
        greet = [(None, r + near), (None, across)]
    else:
        channels = [
            (has_up, -1, has_down, r + 1, slot(0, 0), slot(-1, 0)),
            (has_down, 1, has_up, r - 1, slot(0, 0), slot(1, 0)),
        ]
        greet = [(has_up, r - 1), (has_down, r + 1)]

    def when(cond, f):
        if cond is None:
            f()
        else:
            pl.when(cond)(f)

    barrier = pltpu.get_barrier_semaphore()
    count = 0
    for cond, other in greet:
        when(cond, lambda other=other: pl.semaphore_signal(
            barrier, inc=1, device_id=(other, c), device_id_type=MESH))
        count = count + (1 if cond is None else cond.astype(jnp.int32))
    for cond, other in ((has_left, c - 1), (has_right, c + 1)):
        when(cond, lambda other=other: pl.semaphore_signal(
            barrier, inc=1, device_id=(r, other), device_id_type=MESH))
        count = count + cond.astype(jnp.int32)

    @pl.loop(0, chunks)
    def _(i):
        for copy in local_copies(i):
            copy.start()

    tissue_copy.wait()
    shifts = []
    for a in (-1, 0, 1):
        for b in (-1, 0, 1):
            s = slot(a, b)
            if (a, b) == (0, 0):
                shifts.append(None)
                continue
            inside = jnp.logical_and(jnp.logical_and(r + a >= 0, r + a < rows),
                                     jnp.logical_and(c + b >= 0, c + b < cols))
            entry = tissue[jnp.clip(r + a, 0, rows - 1), jnp.clip(c + b, 0, cols - 1)]
            live = jnp.where(inside, entry, 0) > 0
            shifts.append(jnp.where(live, jnp.float32(0), jnp.float32(-jnp.inf)))

            @pl.when(jnp.logical_not(inside))
            def _():
                @pl.loop(0, chunks)
                def _(i):
                    kv[i, :, s] = jnp.zeros((2, tokens, LANES), kv.dtype)

    pl.semaphore_wait(barrier, count)

    def row_copy(ch, i):
        _, _, _, target, source, landing = channels[ch]
        return pltpu.make_async_remote_copy(
            src_ref=part(i, source), dst_ref=part(i, landing),
            send_sem=row_send.at[ch, i], recv_sem=row_recv.at[ch, i],
            device_id=(target, c), device_id_type=MESH)

    def col_copy(direction, which, i):
        a = 0 if which == 0 else channels[which - 1][1]
        b = -1 if direction == 0 else 1
        return pltpu.make_async_remote_copy(
            src_ref=part(i, slot(a, 0)), dst_ref=part(i, slot(a, b)),
            send_sem=col_send.at[direction, which, i], recv_sem=col_recv.at[direction, which, i],
            device_id=(r, c - b), device_id_type=MESH)

    def row_starts(i):
        for ch in (0, 1):
            when(channels[ch][2], lambda: row_copy(ch, i).start())

    def col_sends(which, i):
        when(has_right, lambda: col_copy(0, which, i).start())
        when(has_left, lambda: col_copy(1, which, i).start())

    depth = ROW_DEPTH if ring else chunks

    @pl.loop(0, chunks)
    def _(i):
        for copy in local_copies(i)[:2]:
            copy.wait()
        kv[i, 1, 4] = raw[1, i].T

        @pl.when(i < depth)
        def _():
            if ring:
                row_copy(0, i).start()
            else:
                row_starts(i)

        pl.when(i < COL_DEPTH)(lambda: col_sends(0, i))

    low = lax.broadcasted_iota(jnp.int32, (LANES, tokens), 0) < HDIM

    @pl.loop(0, chunks)
    def _(i):
        local_copies(i)[2].wait()
        q = (raw[0, i] * jnp.bfloat16(HDIM ** -0.5)).T
        zero = jnp.zeros_like(q)
        qt[i, :, :tokens] = jnp.where(low, q, zero)
        qt[i, :, tokens:] = jnp.where(low, zero, q)

    def first(i):
        def step():
            row_copy(0, i).wait_recv()
            if ring:
                when(channels[1][2], lambda: row_copy(1, i).start())
                pl.when(i + depth < chunks)(lambda: row_copy(0, i + depth).start())
            col_sends(1, i)
        when(channels[0][0], step)
        pl.when(i + COL_DEPTH < chunks)(lambda: col_sends(0, i + COL_DEPTH))

    def second(i):
        def step():
            row_copy(1, i).wait_recv()
            col_sends(2, i)
        when(channels[1][0], step)

    def forward(i):
        first(i)
        pl.when(i > 0)(lambda: second(i - 1))

    own = tissue[r, c].astype(jnp.float32)
    own = tissue[r, c].astype(jnp.float32)

    def arrive(i):
        for direction, cond in ((0, has_left), (1, has_right)):
            for which in (0, 1, 2):
                there = cond
                if which and channels[which - 1][0] is not None:
                    there = jnp.logical_and(cond, channels[which - 1][0])
                when(there, lambda: col_copy(direction, which, i).wait_recv())

    def attend(i):
        queries = qt[i]
        scores = []
        for s, shift in enumerate(shifts):
            tile = jnp.dot(kv[i, 0, s], queries, preferred_element_type=jnp.float32)
            scores.append(tile if shift is None else tile + shift)
        top = jnp.max(functools.reduce(jnp.maximum, scores), axis=0, keepdims=True)
        weights = [jnp.exp(tile - top) for tile in scores]
        totals = jnp.sum(functools.reduce(jnp.add, weights), axis=0, keepdims=True)
        rounded = jnp.concatenate([tile.astype(jnp.bfloat16) for tile in weights], axis=0)
        values = jnp.concatenate([kv[i, 1, s] for s in range(9)], axis=1)
        mixed = jnp.dot(values, rounded, preferred_element_type=jnp.float32)
        mixed = mixed / totals * own
        mixed = jnp.concatenate([mixed[:HDIM, :tokens], mixed[HDIM:, tokens:]], axis=0)
        out_ref[0, 0, :, lanes(i)] = mixed.T.astype(out_ref.dtype)

    def compute(i):
        arrive(i)
        attend(i)

    @pl.loop(0, LAG)
    def _(i):
        forward(i)

    @pl.loop(LAG, chunks)
    def _(i):
        forward(i)
        when(inner if ring else None, lambda: compute(i - LAG))

    second(chunks - 1)

    begin = jnp.where(inner, (chunks - LAG) // 2, 0) if ring else (chunks - LAG) // 2

    @pl.loop(begin, chunks // 2)
    def _(i):
        arrive(2 * i)
        arrive(2 * i + 1)
        attend(2 * i)
        attend(2 * i + 1)

    @pl.loop(0, chunks)
    def _(i):
        for ch in (0, 1):
            when(channels[ch][2], lambda: row_copy(ch, i).wait_send())
        for which in (0, 1, 2):
            for direction, cond in ((0, has_right), (1, has_left)):
                there = cond
                if which and channels[which - 1][0] is not None:
                    there = jnp.logical_and(cond, channels[which - 1][0])
                when(there, lambda: col_copy(direction, which, i).wait_send())


def on_device(rows, cols, query_states, key_states, value_states, tissue_map):
    _, _, tokens, features = query_states.shape
    chunks = features // LANES
    in_hbm = pl.BlockSpec(memory_space=pltpu.HBM)
    return pl.pallas_call(
        functools.partial(kernel, rows, cols),
        out_shape=pltpu.VMEM(query_states.shape, jnp.bfloat16),
        in_specs=[in_hbm] * 4,
        out_specs=pl.BlockSpec(memory_space=pltpu.VMEM),
        scratch_shapes=[
            pltpu.VMEM((chunks, 2, 9, tokens, LANES), jnp.bfloat16),
            pltpu.VMEM((2, chunks, tokens, LANES), jnp.bfloat16),
            pltpu.VMEM((chunks, LANES, 2 * tokens), jnp.bfloat16),
            pltpu.SMEM(tissue_map.shape, jnp.int32),
            pltpu.SemaphoreType.DMA((3, chunks)),
            pltpu.SemaphoreType.DMA,
            pltpu.SemaphoreType.DMA((2, chunks)),
            pltpu.SemaphoreType.DMA((2, chunks)),
            pltpu.SemaphoreType.DMA((2, 3, chunks)),
            pltpu.SemaphoreType.DMA((2, 3, chunks)),
        ],
        compiler_params=pltpu.CompilerParams(
            collective_id=0, has_side_effects=True, vmem_limit_bytes=60 * 1024 * 1024),
        cost_estimate=pl.CostEstimate(
            flops=4 * 9 * tokens * tokens * features, bytes_accessed=8 * tokens * features,
            transcendentals=9 * tokens * tokens * features // HDIM),
        name="neighbourhood",
    )(tissue_map, query_states, key_states, value_states)


def solution(mesh):
    return jax.shard_map(
        functools.partial(on_device, mesh.shape["row"], mesh.shape["col"]),
        mesh=mesh,
        in_specs=(
            P("row", "col", None, None),
            P("row", "col", None, None),
            P("row", "col", None, None),
            P(),
        ),
        out_specs=P("row", "col", None, None),
        check_vma=False,
    )
```

```python
import functools

import jax
import jax.numpy as jnp
from jax import lax
from jax.experimental import pallas as pl
from jax.experimental.pallas import tpu as pltpu
from jax.sharding import PartitionSpec as P

HDIM = 64
LANES = 128
MESH = pl.DeviceIdType.MESH
LAG = 5
ROW_DEPTH = 2
COL_DEPTH = 6


def kernel(rows, cols, tissue_hbm, q_hbm, k_hbm, v_hbm, out_ref, kv, raw, qt, tissue, local_sem,
           tissue_sem, row_send, row_recv, col_send, col_recv):
    chunks, _, _, tokens, _ = kv.shape
    r, c = lax.axis_index("row"), lax.axis_index("col")
    ring = rows == 4
    has_up, has_down = r > 0, r < rows - 1
    has_left, has_right = c > 0, c < cols - 1
    slot = lambda a, b: (a + 1) * 3 + b + 1
    part = lambda i, s: kv.at[i, :, s]

    def lanes(i):
        return pl.ds(pl.multiple_of(i * LANES, LANES), LANES)

    def local_copies(i):
        return [
            pltpu.make_async_copy(k_hbm.at[0, 0, :, lanes(i)], kv.at[i, 0, 4], local_sem.at[0, i]),
            pltpu.make_async_copy(v_hbm.at[0, 0, :, lanes(i)], raw.at[1, i], local_sem.at[1, i]),
            pltpu.make_async_copy(q_hbm.at[0, 0, :, lanes(i)], raw.at[0, i], local_sem.at[2, i]),
        ]

    tissue_copy = pltpu.make_async_copy(tissue_hbm, tissue, tissue_sem)
    tissue_copy.start()

    if ring:
        near = 1 - 2 * lax.rem(r, 2)
        outer = jnp.logical_or(r == 0, r == 3)
        inner = jnp.logical_and(r > 0, r < 3)
        across = jnp.where(r < 2, r + 2, r - 2)
        channels = [
            (None, near, None, r + near, slot(0, 0), slot(-near, 0)),
            (inner, -near, outer, across, slot(near, 0), slot(-near, 0)),
        ]
        greet = [(None, r + near), (None, across)]
    else:
        channels = [
            (has_up, -1, has_down, r + 1, slot(0, 0), slot(-1, 0)),
            (has_down, 1, has_up, r - 1, slot(0, 0), slot(1, 0)),
        ]
        greet = [(has_up, r - 1), (has_down, r + 1)]

    def when(cond, f):
        if cond is None:
            f()
        else:
            pl.when(cond)(f)

    barrier = pltpu.get_barrier_semaphore()
    count = 0
    for cond, other in greet:
        when(cond, lambda other=other: pl.semaphore_signal(
            barrier, inc=1, device_id=(other, c), device_id_type=MESH))
        count = count + (1 if cond is None else cond.astype(jnp.int32))
    for cond, other in ((has_left, c - 1), (has_right, c + 1)):
        when(cond, lambda other=other: pl.semaphore_signal(
            barrier, inc=1, device_id=(r, other), device_id_type=MESH))
        count = count + cond.astype(jnp.int32)

    @pl.loop(0, chunks)
    def _(i):
        for copy in local_copies(i):
            copy.start()

    tissue_copy.wait()
    shifts = []
    for a in (-1, 0, 1):
        for b in (-1, 0, 1):
            s = slot(a, b)
            if (a, b) == (0, 0):
                shifts.append(None)
                continue
            inside = jnp.logical_and(jnp.logical_and(r + a >= 0, r + a < rows),
                                     jnp.logical_and(c + b >= 0, c + b < cols))
            entry = tissue[jnp.clip(r + a, 0, rows - 1), jnp.clip(c + b, 0, cols - 1)]
            live = jnp.where(inside, entry, 0) > 0
            shifts.append(jnp.where(live, jnp.float32(0), jnp.float32(-jnp.inf)))

            @pl.when(jnp.logical_not(inside))
            def _():
                @pl.loop(0, chunks)
                def _(i):
                    kv[i, :, s] = jnp.zeros((2, tokens, LANES), kv.dtype)

    pl.semaphore_wait(barrier, count)

    def row_copy(ch, i):
        _, _, _, target, source, landing = channels[ch]
        return pltpu.make_async_remote_copy(
            src_ref=part(i, source), dst_ref=part(i, landing),
            send_sem=row_send.at[ch, i], recv_sem=row_recv.at[ch, i],
            device_id=(target, c), device_id_type=MESH)

    def col_copy(direction, which, i):
        a = 0 if which == 0 else channels[which - 1][1]
        b = -1 if direction == 0 else 1
        return pltpu.make_async_remote_copy(
            src_ref=part(i, slot(a, 0)), dst_ref=part(i, slot(a, b)),
            send_sem=col_send.at[direction, which, i], recv_sem=col_recv.at[direction, which, i],
            device_id=(r, c - b), device_id_type=MESH)

    def row_starts(i):
        for ch in (0, 1):
            when(channels[ch][2], lambda: row_copy(ch, i).start())

    def col_sends(which, i):
        when(has_right, lambda: col_copy(0, which, i).start())
        when(has_left, lambda: col_copy(1, which, i).start())

    depth = ROW_DEPTH if ring else chunks

    @pl.loop(0, chunks)
    def _(i):
        for copy in local_copies(i)[:2]:
            copy.wait()
        kv[i, 1, 4] = raw[1, i].T

        @pl.when(i < depth)
        def _():
            if ring:
                row_copy(0, i).start()
            else:
                row_starts(i)

        pl.when(i < COL_DEPTH)(lambda: col_sends(0, i))

    low = lax.broadcasted_iota(jnp.int32, (LANES, tokens), 0) < HDIM

    @pl.loop(0, chunks)
    def _(i):
        local_copies(i)[2].wait()
        q = (raw[0, i] * jnp.bfloat16(HDIM ** -0.5)).T
        zero = jnp.zeros_like(q)
        qt[i, :, :tokens] = jnp.where(low, q, zero)
        qt[i, :, tokens:] = jnp.where(low, zero, q)

    def first(i):
        def step():
            row_copy(0, i).wait_recv()
            if ring:
                when(channels[1][2], lambda: row_copy(1, i).start())
                pl.when(i + depth < chunks)(lambda: row_copy(0, i + depth).start())
            col_sends(1, i)
        when(channels[0][0], step)
        pl.when(i + COL_DEPTH < chunks)(lambda: col_sends(0, i + COL_DEPTH))

    def second(i):
        def step():
            row_copy(1, i).wait_recv()
            col_sends(2, i)
        when(channels[1][0], step)

    def forward(i):
        first(i)
        pl.when(i > 0)(lambda: second(i - 1))

    own = tissue[r, c].astype(jnp.float32)
    own = tissue[r, c].astype(jnp.float32)

    def compute(i):
        for direction, cond in ((0, has_left), (1, has_right)):
            for which in (0, 1, 2):
                there = cond
                if which and channels[which - 1][0] is not None:
                    there = jnp.logical_and(cond, channels[which - 1][0])
                when(there, lambda: col_copy(direction, which, i).wait_recv())
        queries = qt[i]
        scores = []
        for s, shift in enumerate(shifts):
            tile = jnp.dot(kv[i, 0, s], queries, preferred_element_type=jnp.float32)
            scores.append(tile if shift is None else tile + shift)
        top = jnp.max(functools.reduce(jnp.maximum, scores), axis=0, keepdims=True)
        weights = [jnp.exp(tile - top) for tile in scores]
        totals = jnp.sum(functools.reduce(jnp.add, weights), axis=0, keepdims=True)
        rounded = jnp.concatenate([tile.astype(jnp.bfloat16) for tile in weights], axis=0)
        values = jnp.concatenate([kv[i, 1, s] for s in range(9)], axis=1)
        mixed = jnp.dot(values, rounded, preferred_element_type=jnp.float32)
        mixed = mixed / totals * own
        mixed = jnp.concatenate([mixed[:HDIM, :tokens], mixed[HDIM:, tokens:]], axis=0)
        out_ref[0, 0, :, lanes(i)] = mixed.T.astype(out_ref.dtype)

    @pl.loop(0, LAG)
    def _(i):
        forward(i)

    @pl.loop(LAG, chunks)
    def _(i):
        forward(i)
        when(inner if ring else None, lambda: compute(i - LAG))

    second(chunks - 1)

    begin = jnp.where(inner, chunks - LAG, 0) if ring else chunks - LAG

    @pl.loop(begin, chunks)
    def _(i):
        compute(i)

    @pl.loop(0, chunks)
    def _(i):
        for ch in (0, 1):
            when(channels[ch][2], lambda: row_copy(ch, i).wait_send())
        for which in (0, 1, 2):
            for direction, cond in ((0, has_right), (1, has_left)):
                there = cond
                if which and channels[which - 1][0] is not None:
                    there = jnp.logical_and(cond, channels[which - 1][0])
                when(there, lambda: col_copy(direction, which, i).wait_send())


def on_device(rows, cols, query_states, key_states, value_states, tissue_map):
    _, _, tokens, features = query_states.shape
    chunks = features // LANES
    in_hbm = pl.BlockSpec(memory_space=pltpu.HBM)
    return pl.pallas_call(
        functools.partial(kernel, rows, cols),
        out_shape=pltpu.VMEM(query_states.shape, jnp.bfloat16),
        in_specs=[in_hbm] * 4,
        out_specs=pl.BlockSpec(memory_space=pltpu.VMEM),
        scratch_shapes=[
            pltpu.VMEM((chunks, 2, 9, tokens, LANES), jnp.bfloat16),
            pltpu.VMEM((2, chunks, tokens, LANES), jnp.bfloat16),
            pltpu.VMEM((chunks, LANES, 2 * tokens), jnp.bfloat16),
            pltpu.SMEM(tissue_map.shape, jnp.int32),
            pltpu.SemaphoreType.DMA((3, chunks)),
            pltpu.SemaphoreType.DMA,
            pltpu.SemaphoreType.DMA((2, chunks)),
            pltpu.SemaphoreType.DMA((2, chunks)),
            pltpu.SemaphoreType.DMA((2, 3, chunks)),
            pltpu.SemaphoreType.DMA((2, 3, chunks)),
        ],
        compiler_params=pltpu.CompilerParams(
            collective_id=0, has_side_effects=True, vmem_limit_bytes=60 * 1024 * 1024),
        cost_estimate=pl.CostEstimate(
            flops=4 * 9 * tokens * tokens * features, bytes_accessed=8 * tokens * features,
            transcendentals=9 * tokens * tokens * features // HDIM),
        name="neighbourhood",
    )(tissue_map, query_states, key_states, value_states)


def solution(mesh):
    return jax.shard_map(
        functools.partial(on_device, mesh.shape["row"], mesh.shape["col"]),
        mesh=mesh,
        in_specs=(
            P("row", "col", None, None),
            P("row", "col", None, None),
            P("row", "col", None, None),
            P(),
        ),
        out_specs=P("row", "col", None, None),
        check_vma=False,
    )
```
